32 devices in a mesh: space: 4 (over y, x), spin: 2 (over core), cons: 4 (over z).
Axes of the slice: x: 2, y: 2, z: 4, core: 2. Of those that a mesh axis runs over, the one named last changes fastest.
Arguments:
- eigvecs: bfloat16 [2, 2, 256, 7680], P(None, None, None, 'space'), may hold values from -0.0625 to 0.0625
- solutions: bfloat16 [2, 2, 4, 256, 7680], P(None, None, 'spin', 'cons', 'space'), may hold values from -6 to 6
- elementals: bfloat16 [8, 2, 256, 256], replicated, may hold values from -0.375 to 0.375
- op_list: int32 [32, 16, 4], P(('space', 'spin', 'cons')), may hold values from 0 to 7, as said below
- live_count: int32 [32], P(('space', 'spin', 'cons')), may hold values from 1 to 16, as said below
Outputs:
- blocks: bfloat16 [2, 512, 256, 256], P(None, ('space', 'spin', 'cons'))
The draws below stay inside these ranges and needn't reach their ends.
Inputs may be any that keep to these rules, and one draw needn't show every extreme that they name: `op_list`: columns hold an elemental in 0 to 7, two sink spins in 0 to 3 and a sink slice in 0 to 1; slots at or beyond an owner's live count hold arbitrary entries of that kind. `live_count`: some owner has all 16 slots live.
All inputs are finite; a program needn't handle non-finite values.
Results may differ from the reference program's by a relative error of at most 0.0064.
Values may be sent and summed in bfloat16 or wider, within the bound.
No kernel may reach another device: no remote copies, remote signals or barrier semaphores. Data moves between devices by JAX's collectives and lax.ppermute only.
A program may use at most 128 MiB of HBM per device.

```python
import jax
import jax.numpy as jnp
from jax import lax

NEV = 256
NT = 2
NELEM = 8
SLOTS = 16
ROWS = 7680
OWNERS = 32


def draw_op_list(key, part):
    keys = jax.random.split(key, 4)
    elem = jax.random.randint(keys[0], (OWNERS, SLOTS), 0, NELEM)
    spin_a = jax.random.randint(keys[1], (OWNERS, SLOTS), 0, 4)
    spin_b = jax.random.randint(keys[2], (OWNERS, SLOTS), 0, 4)
    slice_t = jax.random.randint(keys[3], (OWNERS, SLOTS), 0, NT)
    first = (jnp.arange(OWNERS)[:, None] == 0) & (jnp.arange(SLOTS)[None, :] == 0)
    elem = jnp.where(first, NELEM - 1, elem)
    spin_a = jnp.where(first, 0, spin_a)
    spin_b = jnp.where(first, 3, spin_b)
    return jnp.stack([elem, spin_a, spin_b, slice_t], axis=-1).astype(jnp.int32)


def draw_live_count(key, part):
    keys = jax.random.split(key, 2)
    counts = jax.random.randint(keys[0], (OWNERS,), 1, SLOTS + 1)
    fullest = jax.random.randint(keys[1], (), 0, OWNERS)
    counts = jnp.where(jnp.arange(OWNERS) == fullest, SLOTS, counts)
    return counts.astype(jnp.int32)


def block_levels(rng, extent, cuts, smallest, top_value):
    gain = 1.0
    for position, parts in cuts:
        steps = jax.random.uniform(jax.random.fold_in(jax.random.fold_in(rng, 6), position), (parts,), jnp.float32, smallest / len(cuts), top_value / len(cuts))
        gain = gain * jnp.repeat(jnp.exp(steps), extent[position] // parts).reshape((-1,) + (1,) * (len(extent) - 1 - position))
    return gain


def bell_draw(key, extent, scale, bound, pieces=(), held_as=jnp.bfloat16):
    array = jax.random.normal(key, extent, jnp.float32) * scale
    if len(pieces) > 0:
        array = block_levels(key, extent, pieces, -0.22, 0.18) * array
    return jnp.clip(array, min=-bound, max=bound).astype(held_as)


def setup_inputs(seed: int = 0) -> dict:
    key_list = jax.random.split(jax.random.key(seed), 6)
    return {
        "eigvecs": bell_draw(key_list[0], (2, NT, NEV, ROWS), ROWS ** -0.5, 0.0625, ((3, 4),)),
        "solutions": bell_draw(key_list[1], (2, NT, 4, NEV, ROWS), 1.0, 6.0, ((2, 2), (3, 4), (4, 4))),
        "elementals": bell_draw(key_list[2], (NELEM, 2, NEV, NEV), NEV ** -0.5, 0.375),
        "op_list": draw_op_list(jax.random.fold_in(key_list[5], 71), 0),
        "live_count": draw_live_count(jax.random.fold_in(key_list[5], 71), 0),
    }


def contract(left, phi, right):
    prod = jnp.einsum("pik,qkj->pqij", phi.astype(jnp.float32), right.astype(jnp.float32))
    mixed = jnp.stack([prod[0, 0] - prod[1, 1], prod[0, 1] + prod[1, 0]]).astype(jnp.bfloat16)
    prod_two = jnp.einsum("pki,qkj->pqij", left.astype(jnp.float32), mixed.astype(jnp.float32))
    return jnp.stack([prod_two[0, 0] + prod_two[1, 1], prod_two[0, 1] - prod_two[1, 0]]) * (NEV ** -0.5)


def reference(eigvecs, solutions, elementals, op_list, live_count):
    def project(slice_t):
        vecs = eigvecs[:, slice_t].astype(jnp.float32)
        sols = solutions[:, slice_t].astype(jnp.float32)
        prod = jnp.einsum("pir,qsjr->pqsij", vecs, sols)
        return jnp.stack([prod[0, 0] + prod[1, 1], prod[0, 1] - prod[1, 0]])

    tau = lax.map(project, jnp.arange(NT)).astype(jnp.bfloat16)
    flat = jnp.transpose(tau, (1, 0, 2, 3, 4)).reshape(2, NT * 4, NEV, NEV)
    items = op_list.reshape(OWNERS * SLOTS, 4)
    live = (jnp.arange(SLOTS)[None, :] < live_count[:, None]).reshape(OWNERS * SLOTS)

    def one_item(packed):
        item, keep = packed
        left = flat[:, item[3] * 4 + item[1]]
        right = flat[:, item[3] * 4 + item[2]]
        result = contract(left, elementals[item[0]], right)
        return jnp.where(keep, result, jnp.zeros_like(result)).astype(jnp.bfloat16)

    results = lax.map(one_item, (items, live))
    return jnp.transpose(results, (1, 0, 2, 3))
```

```python
import functools

import jax
import jax.numpy as jnp
from jax import lax
from jax.experimental import pallas as pl
from jax.experimental.pallas import tpu as pltpu
from jax.sharding import PartitionSpec as P

NT_DOT = (((1,), (1,)), ((), ()))
NN_DOT = (((1,), (0,)), ((), ()))


def partners(n):
    if n & (n - 1) == 0:
        return [[(i, i ^ s) for i in range(n)] for s in range(n)]
    return [[(i, (i + s) % n) for i in range(n)] for s in range(n)]


def partner(index, step, n):
    if n & (n - 1) == 0:
        return index ^ step
    return lax.rem(index - step + n, n)


def target(index, step, n):
    if n & (n - 1) == 0:
        return index ^ step
    return lax.rem(index + step, n)


def depth_cuts(depth):
    half = max(256, (depth // 2 + 255) // 256 * 256)
    return [(0, half), (half, depth)] if half < depth else [(0, depth)]


def partial_kernel(n_space, cuts, pos_ref, v_ref, s_ref, *rest):
    outs = rest[:n_space]
    v_buf, s_buf, acc, in_sem, out_sem = rest[n_space:]
    _, nt, nev, _ = v_ref.shape
    _, _, nsp, nj, _ = s_ref.shape
    copies = []
    for t in range(nt):
        for c, (lo, hi) in enumerate(cuts):
            pair = (
                pltpu.make_async_copy(
                    v_ref.at[:, t, :, lo:hi], v_buf.at[:, t, :, lo:hi], in_sem.at[t, c, 0]
                ),
                pltpu.make_async_copy(
                    s_ref.at[:, t, :, :, lo:hi], s_buf.at[:, t, :, :, lo:hi], in_sem.at[t, c, 1]
                ),
            )
            for copy in pair:
                copy.start()
            copies.append(pair)
    for t in range(nt):
        total = None
        for c, (lo, hi) in enumerate(cuts):
            for copy in copies[t * len(cuts) + c]:
                copy.wait()
            vr, vi = v_buf[0, t, :, lo:hi], v_buf[1, t, :, lo:hi]
            sr = s_buf[0, t, :, :, lo:hi].reshape(nsp * nj, hi - lo)
            si = s_buf[1, t, :, :, lo:hi].reshape(nsp * nj, hi - lo)
            one = lax.dot_general(
                jnp.concatenate([sr, si]), vr, NT_DOT, preferred_element_type=jnp.float32
            )
            two = lax.dot_general(
                jnp.concatenate([si, -sr]), vi, NT_DOT, preferred_element_type=jnp.float32
            )
            total = one + two if total is None else total + one + two
        total = total.reshape(2, nsp, nj, nev)
        for sp in range(nsp):
            for p in range(2):
                start = ((t * nsp + sp) * 2 + p) * nj
                acc[start : start + nj, :] = total[p, sp]
    chunk = acc.shape[0] // n_space
    me = pos_ref[0]
    writes = []
    for s in range(n_space):
        who = target(me, s, n_space)
        copy = pltpu.make_async_copy(
            acc.at[pl.ds(pl.multiple_of(who * chunk, chunk), chunk)], outs[s], out_sem.at[s]
        )
        copy.start()
        writes.append(copy)
    for copy in writes:
        copy.wait()


def partial_taus(pos, eigvecs, solutions, n_space):
    _, nt, nev, depth = eigvecs.shape
    _, _, nsp, nj, _ = solutions.shape
    rows = nt * nsp * 2 * nj
    cuts = depth_cuts(depth)
    chunk = jax.ShapeDtypeStruct((rows // n_space, nev), jnp.float32)
    return pl.pallas_call(
        functools.partial(partial_kernel, n_space, cuts),
        out_shape=[chunk] * n_space,
        in_specs=[
            pl.BlockSpec(memory_space=pltpu.SMEM),
            pl.BlockSpec(memory_space=pl.ANY),
            pl.BlockSpec(memory_space=pl.ANY),
        ],
        out_specs=[pl.BlockSpec(memory_space=pl.ANY)] * n_space,
        scratch_shapes=[
            pltpu.VMEM(eigvecs.shape, eigvecs.dtype),
            pltpu.VMEM(solutions.shape, solutions.dtype),
            pltpu.VMEM((rows, nev), jnp.float32),
            pltpu.SemaphoreType.DMA((nt, len(cuts), 2)),
            pltpu.SemaphoreType.DMA((n_space,)),
        ],
        compiler_params=pltpu.CompilerParams(vmem_limit_bytes=32 * 2**20),
        cost_estimate=pl.CostEstimate(
            flops=4 * rows * nev * depth,
            bytes_accessed=2 * (eigvecs.size + solutions.size) + 4 * rows * nev,
            transcendentals=0,
        ),
    )(pos, eigvecs, solutions)


def contract_kernel(layout, per_chunk, pos_ref, item_ref, live_ref, elem_ref, *rest):
    n_space, n_spin, n_cons, nt, nsp, nj = layout
    n_parts = n_space * n_spin
    parts, out_ref = rest[:n_parts], rest[n_parts]
    tau, elems, outs, tau_sem, elem_sem, out_sem = rest[n_parts + 1 :]
    unit, nev = tau.shape[-2:]
    slots = out_ref.shape[1]
    space, spin, cons = pos_ref[0], pos_ref[1], pos_ref[2]
    loads = [pltpu.make_async_copy(elem_ref, elems, elem_sem)]
    for n, part in enumerate(parts):
        loads.append(pltpu.make_async_copy(part, tau.at[n], tau_sem.at[n]))
    for copy in loads:
        copy.start()
    for copy in loads:
        copy.wait()

    def matrix(t, a, p):
        owner = a // nsp
        first = ((t * nsp + a % nsp) * 2 + p) * (nj // unit)
        rows = []
        for z in range(n_cons):
            z_step = step_from(z, cons, n_cons)
            for k in range(nj // unit):
                where = first + k
                part = step_from(owner, spin, n_spin) * n_space + step_from(
                    where // per_chunk, space, n_space
                )
                rows.append(tau[part, z_step * per_chunk + where % per_chunk])
        return jnp.concatenate(rows)

    def write(k):
        return pltpu.make_async_copy(outs.at[k], out_ref.at[:, k], out_sem.at[k])

    def one_slot(k, carry):
        @pl.when(k < live_ref[0])
        def _():
            e, a, b, t = (item_ref[4 * k + n] for n in range(4))
            er, ei = elems[e, 0], elems[e, 1]
            tr, ti = matrix(t, b, 0), matrix(t, b, 1)
            dot = functools.partial(lax.dot_general, preferred_element_type=jnp.float32)
            xr = (dot(er, tr, NT_DOT) + dot(-ei, ti, NT_DOT)).astype(jnp.bfloat16)
            xi = (dot(er, ti, NT_DOT) + dot(ei, tr, NT_DOT)).astype(jnp.bfloat16)
            ar, ai = matrix(t, a, 0), matrix(t, a, 1)
            scale = nev ** (-0.5)
            outs[k, 0] = ((dot(ar, xr, NN_DOT) + dot(ai, xi, NN_DOT)) * scale).astype(jnp.bfloat16)
            outs[k, 1] = ((dot(ar, xi, NN_DOT) + dot(-ai, xr, NN_DOT)) * scale).astype(jnp.bfloat16)

        @pl.when(k >= live_ref[0])
        def _():
            outs[k] = jnp.zeros(outs.shape[1:], outs.dtype)

        write(k).start()
        return carry

    lax.fori_loop(0, slots, one_slot, 0)
    for k in range(slots):
        write(k).wait()


def step_from(sender, me, n):
    if n & (n - 1) == 0:
        return sender ^ me
    return lax.rem(me - sender + n, n)


def contract(pos, items, live, elementals, parts, layout):
    n_space, n_spin, n_cons, nt, nsp, nj = layout
    slots = items.shape[0]
    nev = elementals.shape[-1]
    chunk = parts[0].shape[-2]
    unit = min(chunk, nj)
    parts = [part.reshape(n_cons * chunk // unit, unit, nev) for part in parts]
    return pl.pallas_call(
        functools.partial(contract_kernel, layout, chunk // unit),
        out_shape=jax.ShapeDtypeStruct((2, slots, nev, nev), jnp.bfloat16),
        in_specs=[pl.BlockSpec(memory_space=pltpu.SMEM)] * 3
        + [pl.BlockSpec(memory_space=pl.ANY)] * (1 + len(parts)),
        out_specs=pl.BlockSpec(memory_space=pl.ANY),
        scratch_shapes=[
            pltpu.VMEM((len(parts),) + parts[0].shape, jnp.bfloat16),
            pltpu.VMEM(elementals.shape, jnp.bfloat16),
            pltpu.VMEM((slots, 2, nev, nev), jnp.bfloat16),
            pltpu.SemaphoreType.DMA((len(parts),)),
            pltpu.SemaphoreType.DMA,
            pltpu.SemaphoreType.DMA((slots,)),
        ],
        compiler_params=pltpu.CompilerParams(vmem_limit_bytes=32 * 2**20),
        cost_estimate=pl.CostEstimate(
            flops=16 * slots * nev**3,
            bytes_accessed=2 * (elementals.size + 2 * slots * nev * nev),
            transcendentals=0,
        ),
    )(pos, items.reshape(-1), live, elementals, *parts)


def body(eigvecs, solutions, elementals, op_list, live_count):
    n_space, n_spin, n_cons = (lax.axis_size(a) for a in ("space", "spin", "cons"))
    pos = jnp.stack([lax.axis_index(a) for a in ("space", "spin", "cons")]).astype(jnp.int32)
    _, nt, nsp, nj, _ = solutions.shape
    sends = partial_taus(pos, eigvecs, solutions, n_space)
    space_steps, spin_steps, cons_steps = partners(n_space), partners(n_spin), partners(n_cons)
    got = [sends[0]] + [
        lax.ppermute(sends[s], "space", space_steps[s]) for s in range(1, n_space)
    ]
    mine = functools.reduce(jnp.add, got).astype(jnp.bfloat16)
    column = jnp.stack(
        [mine] + [lax.ppermute(mine, "cons", cons_steps[s]) for s in range(1, n_cons)]
    )
    plane = [column] + [
        lax.ppermute(column, "space", space_steps[s]) for s in range(1, n_space)
    ]
    parts = list(plane)
    for s in range(1, n_spin):
        parts += [lax.ppermute(part, "spin", spin_steps[s]) for part in plane]
    layout = (n_space, n_spin, n_cons, nt, nsp, nj)
    return contract(pos, op_list[0], live_count, elementals, parts, layout)


def solution(mesh):
    return jax.shard_map(
        body,
        mesh=mesh,
        in_specs=(
            P(None, None, None, "space"),
            P(None, None, "spin", "cons", "space"),
            P(),
            P(("space", "spin", "cons"), None, None),
            P(("space", "spin", "cons")),
        ),
        out_specs=P(None, ("space", "spin", "cons"), None, None),
        check_vma=False,
    )
```

```python
import functools
import math

import jax
import jax.numpy as jnp
from jax import lax
from jax.experimental import pallas as pl
from jax.experimental.pallas import tpu as pltpu
from jax.sharding import PartitionSpec as P

NT_DOT = (((1,), (1,)), ((), ()))
NN_DOT = (((1,), (0,)), ((), ()))


dot = functools.partial(lax.dot_general, preferred_element_type=jnp.float32)


def partners(n):
    if n & (n - 1) == 0:
        return [[(i, i ^ s) for i in range(n)] for s in range(n)]
    return [[(i, (i + s) % n) for i in range(n)] for s in range(n)]


def partner(index, step, n):
    if n & (n - 1) == 0:
        return index ^ step
    return lax.rem(index - step + n, n)


def target(index, step, n):
    if n & (n - 1) == 0:
        return index ^ step
    return lax.rem(index + step, n)


def depth_cuts(depth):
    half = max(256, (depth // 2 + 255) // 256 * 256)
    return [(0, half), (half, depth)] if half < depth else [(0, depth)]


def partial_kernel(n_space, cuts, pos_ref, v_ref, s_ref, *rest):
    outs = rest[:n_space]
    v_buf, s_buf, acc, in_sem = rest[n_space:]
    _, nt, nev, _ = v_ref.shape
    _, _, nsp, nj, _ = s_ref.shape
    copies = []
    for t in range(nt):
        for c, (lo, hi) in enumerate(cuts):
            group = []
            for p in range(2):
                group += [
                    pltpu.make_async_copy(
                        v_ref.at[p, t, :, lo:hi], v_buf.at[p, t, :, lo:hi], in_sem.at[t, c, 2 * p]
                    ),
                    pltpu.make_async_copy(
                        s_ref.at[p, t, :, :, lo:hi],
                        s_buf.at[p, t, :, :, lo:hi],
                        in_sem.at[t, c, 2 * p + 1],
                    ),
                ]
            for copy in group:
                copy.start()
            copies.append(group)
    for t in range(nt):
        total = None
        for c, (lo, hi) in enumerate(cuts):
            for copy in copies[t * len(cuts) + c]:
                copy.wait()
            vr, vi = v_buf[0, t, :, lo:hi], v_buf[1, t, :, lo:hi]
            sr = s_buf[0, t, :, :, lo:hi].reshape(nsp * nj, hi - lo)
            si = s_buf[1, t, :, :, lo:hi].reshape(nsp * nj, hi - lo)
            both = dot(jnp.concatenate([sr, si]), vr, NT_DOT) + dot(
                jnp.concatenate([si, -sr]), vi, NT_DOT
            )
            total = both if total is None else total + both
        total = total.reshape(2, nsp, nj, nev)
        for sp in range(nsp):
            for p in range(2):
                start = ((t * nsp + sp) * 2 + p) * nj
                acc[start : start + nj, :] = total[p, sp]
    chunk = acc.shape[0] // n_space
    me = pos_ref[0]
    for s in range(n_space):
        first = pl.multiple_of(target(me, s, n_space) * chunk, chunk)
        outs[s][...] = acc[pl.ds(first, chunk), :].astype(outs[s].dtype)


def partial_taus(pos, eigvecs, solutions, n_space, send_type):
    _, nt, nev, depth = eigvecs.shape
    _, _, nsp, nj, _ = solutions.shape
    rows = nt * nsp * 2 * nj
    cuts = depth_cuts(depth)
    chunk = (rows // n_space, nev)
    return pl.pallas_call(
        functools.partial(partial_kernel, n_space, cuts),
        out_shape=[pltpu.VMEM(chunk, jnp.float32)] + [pltpu.VMEM(chunk, send_type)] * (n_space - 1),
        in_specs=[
            pl.BlockSpec(memory_space=pltpu.SMEM),
            pl.BlockSpec(memory_space=pl.ANY),
            pl.BlockSpec(memory_space=pl.ANY),
        ],
        out_specs=[pl.BlockSpec(memory_space=pltpu.VMEM)] * n_space,
        scratch_shapes=[
            pltpu.VMEM(eigvecs.shape, eigvecs.dtype),
            pltpu.VMEM(solutions.shape, solutions.dtype),
            pltpu.VMEM((rows, nev), jnp.float32),
            pltpu.SemaphoreType.DMA((nt, len(cuts), 4)),
        ],
        compiler_params=pltpu.CompilerParams(vmem_limit_bytes=32 * 2**20),
        cost_estimate=pl.CostEstimate(
            flops=4 * rows * nev * depth,
            bytes_accessed=2 * (eigvecs.size + solutions.size) + 4 * rows * nev,
            transcendentals=0,
        ),
    )(
        pos,
        pltpu.with_memory_space_constraint(eigvecs, pltpu.HBM),
        pltpu.with_memory_space_constraint(solutions, pltpu.HBM),
    )


def contract_kernel(layout, per_chunk, group, pos_ref, item_ref, live_ref, elems, *rest):
    n_space, n_spin, n_cons, nt, nsp, nj = layout
    n_parts = n_space * n_spin
    parts, out_ref = rest[:n_parts], rest[n_parts]
    tau, outs, mid, tau_sem, out_sem = rest[n_parts + 1 :]
    unit, nev = tau.shape[-2:]
    slots = out_ref.shape[1]
    scale = nev ** (-0.5)
    space, spin, cons = pos_ref[0], pos_ref[1], pos_ref[2]
    loads = [pltpu.make_async_copy(part, tau.at[n], tau_sem.at[n]) for n, part in enumerate(parts)]
    for copy in loads:
        copy.start()
    for copy in loads:
        copy.wait()

    def matrix(t, a, p):
        first = ((t * nsp + a % nsp) * 2 + p) * (nj // unit)
        rows = []
        for z in range(n_cons):
            z_step = step_from(z, cons, n_cons)
            for k in range(nj // unit):
                where = first + k
                part = step_from(a // nsp, spin, n_spin) * n_space + step_from(
                    where // per_chunk, space, n_space
                )
                rows.append(tau[part, z_step * per_chunk + where % per_chunk])
        return jnp.concatenate(rows)

    def write(k):
        return pltpu.make_async_copy(outs.at[k], out_ref.at[:, k], out_sem.at[k])

    def right_half(u, item):
        e, _, b, t = item
        er, ei = elems[e, 0], elems[e, 1]
        tau_b = jnp.concatenate([matrix(t, b, 0), matrix(t, b, 1)], axis=1)
        real = dot(jnp.concatenate([er, -ei], axis=1), tau_b, NT_DOT)
        imag = dot(jnp.concatenate([ei, er], axis=1), tau_b, NT_DOT)
        mid[u, :nev] = real.astype(mid.dtype)
        mid[u, nev:] = imag.astype(mid.dtype)

    def left_half(u, k, item):
        _, a, _, t = item
        ar, ai = matrix(t, a, 0), matrix(t, a, 1)
        keep = k < live_ref[0]
        real = dot(jnp.concatenate([ar, ai], axis=1), mid[u], NN_DOT)
        imag = dot(jnp.concatenate([-ai, ar], axis=1), mid[u], NN_DOT)
        outs[k, 0] = jnp.where(keep, real * scale, 0.0).astype(outs.dtype)
        outs[k, 1] = jnp.where(keep, imag * scale, 0.0).astype(outs.dtype)

    def one_group(g, carry):
        ks = [g * group + u for u in range(group)]
        items = [tuple(item_ref[4 * k + n] for n in range(4)) for k in ks]
        right_half(0, items[0])
        for u in range(group):
            if u + 1 < group:
                right_half(u + 1, items[u + 1])
            left_half(u, ks[u], items[u])
        for k in ks:
            write(k).start()
        return carry

    def empty_group(g, carry):
        for u in range(group):
            k = g * group + u
            outs[k] = jnp.zeros(outs.shape[1:], outs.dtype)
            write(k).start()
        return carry

    n_groups = slots // group
    used = lax.div(live_ref[0] + group - 1, group)
    lax.fori_loop(0, used, one_group, 0)
    lax.fori_loop(used, n_groups, empty_group, 0)
    for k in range(slots):
        write(k).wait()


def step_from(sender, me, n):
    if n & (n - 1) == 0:
        return sender ^ me
    return lax.rem(me - sender + n, n)


def contract(pos, items, live, elementals, parts, layout):
    n_space, n_spin, n_cons, nt, nsp, nj = layout
    slots = items.shape[0]
    nev = elementals.shape[-1]
    chunk = parts[0].shape[-2]
    unit = min(chunk, nj)
    group = math.gcd(slots, 4)
    parts = [part.reshape(n_cons * chunk // unit, unit, nev) for part in parts]
    return pl.pallas_call(
        functools.partial(contract_kernel, layout, chunk // unit, group),
        out_shape=jax.ShapeDtypeStruct((2, slots, nev, nev), jnp.bfloat16),
        in_specs=[pl.BlockSpec(memory_space=pltpu.SMEM)] * 3
        + [pl.BlockSpec(memory_space=pltpu.VMEM)]
        + [pl.BlockSpec(memory_space=pl.ANY)] * len(parts),
        out_specs=pl.BlockSpec(memory_space=pl.ANY),
        scratch_shapes=[
            pltpu.VMEM((len(parts),) + parts[0].shape, jnp.bfloat16),
            pltpu.VMEM((slots, 2, nev, nev), jnp.bfloat16),
            pltpu.VMEM((group, 2 * nev, nev), jnp.bfloat16),
            pltpu.SemaphoreType.DMA((len(parts),)),
            pltpu.SemaphoreType.DMA((slots,)),
        ],
        compiler_params=pltpu.CompilerParams(vmem_limit_bytes=32 * 2**20),
        cost_estimate=pl.CostEstimate(
            flops=16 * slots * nev**3,
            bytes_accessed=2 * (elementals.size + 2 * slots * nev * nev),
            transcendentals=0,
        ),
    )(
        pos,
        items.reshape(-1),
        live,
        pltpu.with_memory_space_constraint(elementals, pltpu.VMEM),
        *parts,
    )


def body(eigvecs, solutions, elementals, op_list, live_count):
    n_space, n_spin, n_cons = (lax.axis_size(a) for a in ("space", "spin", "cons"))
    pos = jnp.stack([lax.axis_index(a) for a in ("space", "spin", "cons")]).astype(jnp.int32)
    _, nt, nsp, nj, _ = solutions.shape
    sends = partial_taus(pos, eigvecs, solutions, n_space, jnp.float32)
    space_steps, spin_steps, cons_steps = partners(n_space), partners(n_spin), partners(n_cons)
    got = [sends[0]] + [
        lax.ppermute(sends[s], "space", space_steps[s]) for s in range(1, n_space)
    ]
    mine = functools.reduce(jnp.add, got).astype(jnp.bfloat16)
    column = jnp.stack(
        [mine] + [lax.ppermute(mine, "cons", cons_steps[s]) for s in range(1, n_cons)]
    )
    plane = [column] + [
        lax.ppermute(column, "space", space_steps[s]) for s in range(1, n_space)
    ]
    parts = list(plane)
    for s in range(1, n_spin):
        parts += [lax.ppermute(part, "spin", spin_steps[s]) for part in plane]
    layout = (n_space, n_spin, n_cons, nt, nsp, nj)
    return contract(pos, op_list[0], live_count, elementals, parts, layout)


def solution(mesh):
    return jax.shard_map(
        body,
        mesh=mesh,
        in_specs=(
            P(None, None, None, "space"),
            P(None, None, "spin", "cons", "space"),
            P(),
            P(("space", "spin", "cons"), None, None),
            P(("space", "spin", "cons")),
        ),
        out_specs=P(None, ("space", "spin", "cons"), None, None),
        check_vma=False,
    )
```

```python
import functools
import math

import jax
import jax.numpy as jnp
from jax import lax
from jax.experimental import pallas as pl
from jax.experimental.pallas import tpu as pltpu
from jax.sharding import PartitionSpec as P

NT_DOT = (((1,), (1,)), ((), ()))
NN_DOT = (((1,), (0,)), ((), ()))


dot = functools.partial(lax.dot_general, preferred_element_type=jnp.float32)


def partners(n):
    if n & (n - 1) == 0:
        return [[(i, i ^ s) for i in range(n)] for s in range(n)]
    return [[(i, (i + s) % n) for i in range(n)] for s in range(n)]


def partner(index, step, n):
    if n & (n - 1) == 0:
        return index ^ step
    return lax.rem(index - step + n, n)


def target(index, step, n):
    if n & (n - 1) == 0:
        return index ^ step
    return lax.rem(index + step, n)


def depth_cuts(depth):
    half = max(256, (depth // 2 + 255) // 256 * 256)
    return [(0, half), (half, depth)] if half < depth else [(0, depth)]


def partial_kernel(n_space, cuts, pos_ref, v_ref, s_ref, *rest):
    outs = rest[:n_space]
    v_buf, s_buf, acc, in_sem = rest[n_space:]
    _, nt, nev, _ = v_ref.shape
    _, _, nsp, nj, _ = s_ref.shape
    copies = []
    for t in range(nt):
        for c, (lo, hi) in enumerate(cuts):
            group = []
            for p in range(2):
                group += [
                    pltpu.make_async_copy(
                        v_ref.at[p, t, :, lo:hi], v_buf.at[p, t, :, lo:hi], in_sem.at[t, c, 2 * p]
                    ),
                    pltpu.make_async_copy(
                        s_ref.at[p, t, :, :, lo:hi],
                        s_buf.at[p, t, :, :, lo:hi],
                        in_sem.at[t, c, 2 * p + 1],
                    ),
                ]
            for copy in group:
                copy.start()
            copies.append(group)
    for t in range(nt):
        total = None
        for c, (lo, hi) in enumerate(cuts):
            for copy in copies[t * len(cuts) + c]:
                copy.wait()
            vr, vi = v_buf[0, t, :, lo:hi], v_buf[1, t, :, lo:hi]
            sr = s_buf[0, t, :, :, lo:hi].reshape(nsp * nj, hi - lo)
            si = s_buf[1, t, :, :, lo:hi].reshape(nsp * nj, hi - lo)
            both = dot(jnp.concatenate([sr, si]), vr, NT_DOT) + dot(
                jnp.concatenate([si, -sr]), vi, NT_DOT
            )
            total = both if total is None else total + both
        total = total.reshape(2, nsp, nj, nev)
        for sp in range(nsp):
            for p in range(2):
                start = ((t * nsp + sp) * 2 + p) * nj
                acc[start : start + nj, :] = total[p, sp]
    chunk = acc.shape[0] // n_space
    me = pos_ref[0]
    for s in range(n_space):
        first = pl.multiple_of(target(me, s, n_space) * chunk, chunk)
        outs[s][...] = acc[pl.ds(first, chunk), :].astype(outs[s].dtype)


def partial_taus(pos, eigvecs, solutions, n_space, send_type):
    _, nt, nev, depth = eigvecs.shape
    _, _, nsp, nj, _ = solutions.shape
    rows = nt * nsp * 2 * nj
    cuts = depth_cuts(depth)
    chunk = (rows // n_space, nev)
    return pl.pallas_call(
        functools.partial(partial_kernel, n_space, cuts),
        out_shape=[pltpu.VMEM(chunk, jnp.float32)] + [pltpu.VMEM(chunk, send_type)] * (n_space - 1),
        in_specs=[
            pl.BlockSpec(memory_space=pltpu.SMEM),
            pl.BlockSpec(memory_space=pl.ANY),
            pl.BlockSpec(memory_space=pl.ANY),
        ],
        out_specs=[pl.BlockSpec(memory_space=pltpu.VMEM)] * n_space,
        scratch_shapes=[
            pltpu.VMEM(eigvecs.shape, eigvecs.dtype),
            pltpu.VMEM(solutions.shape, solutions.dtype),
            pltpu.VMEM((rows, nev), jnp.float32),
            pltpu.SemaphoreType.DMA((nt, len(cuts), 4)),
        ],
        compiler_params=pltpu.CompilerParams(vmem_limit_bytes=32 * 2**20),
        cost_estimate=pl.CostEstimate(
            flops=4 * rows * nev * depth,
            bytes_accessed=2 * (eigvecs.size + solutions.size) + 4 * rows * nev,
            transcendentals=0,
        ),
    )(
        pos,
        pltpu.with_memory_space_constraint(eigvecs, pltpu.HBM),
        pltpu.with_memory_space_constraint(solutions, pltpu.HBM),
    )


def contract_kernel(layout, per_chunk, group, pos_ref, item_ref, live_ref, elems, *rest):
    n_space, n_spin, n_cons, nt, nsp, nj = layout
    n_parts = n_space * n_spin
    parts, out_ref = rest[:n_parts], rest[n_parts]
    tau, outs, mid, tau_sem, out_sem = rest[n_parts + 1 :]
    unit, nev = tau.shape[-2:]
    slots = out_ref.shape[1]
    scale = nev ** (-0.5)
    space, spin, cons = pos_ref[0], pos_ref[1], pos_ref[2]
    loads = [pltpu.make_async_copy(part, tau.at[n], tau_sem.at[n]) for n, part in enumerate(parts)]
    for copy in loads:
        copy.start()
    for copy in loads:
        copy.wait()

    def matrix(t, a, p):
        first = ((t * nsp + a % nsp) * 2 + p) * (nj // unit)
        rows = []
        for z in range(n_cons):
            z_step = step_from(z, cons, n_cons)
            for k in range(nj // unit):
                where = first + k
                part = step_from(a // nsp, spin, n_spin) * n_space + step_from(
                    where // per_chunk, space, n_space
                )
                rows.append(tau[part, z_step * per_chunk + where % per_chunk])
        return jnp.concatenate(rows)

    def write(k):
        return pltpu.make_async_copy(outs.at[k], out_ref.at[:, k], out_sem.at[k])

    def right_half(u, item):
        e, _, b, t = item
        er, ei = elems[e, 0], elems[e, 1]
        tau_b = jnp.concatenate([matrix(t, b, 0), matrix(t, b, 1)], axis=1)
        real = dot(jnp.concatenate([er, -ei], axis=1), tau_b, NT_DOT)
        imag = dot(jnp.concatenate([ei, er], axis=1), tau_b, NT_DOT)
        mid[u, :nev] = real.astype(mid.dtype)
        mid[u, nev:] = imag.astype(mid.dtype)

    def left_half(u, k, item):
        _, a, _, t = item
        ar, ai = matrix(t, a, 0), matrix(t, a, 1)
        keep = k < live_ref[0]
        real = dot(jnp.concatenate([ar, ai], axis=1), mid[u], NN_DOT)
        imag = dot(jnp.concatenate([-ai, ar], axis=1), mid[u], NN_DOT)
        outs[k, 0] = jnp.where(keep, real * scale, 0.0).astype(outs.dtype)
        outs[k, 1] = jnp.where(keep, imag * scale, 0.0).astype(outs.dtype)

    def one_group(g, carry):
        ks = [g * group + u for u in range(group)]
        items = [tuple(item_ref[4 * k + n] for n in range(4)) for k in ks]
        right_half(0, items[0])
        for u in range(group):
            if u + 1 < group:
                right_half(u + 1, items[u + 1])
            left_half(u, ks[u], items[u])
        for k in ks:
            write(k).start()
        return carry

    def empty_group(g, carry):
        for u in range(group):
            k = g * group + u
            outs[k] = jnp.zeros(outs.shape[1:], outs.dtype)
            write(k).start()
        return carry

    n_groups = slots // group
    used = lax.div(live_ref[0] + group - 1, group)
    lax.fori_loop(0, used, one_group, 0)
    lax.fori_loop(used, n_groups, empty_group, 0)
    for k in range(slots):
        write(k).wait()


def step_from(sender, me, n):
    if n & (n - 1) == 0:
        return sender ^ me
    return lax.rem(me - sender + n, n)


def contract(pos, items, live, elementals, parts, layout):
    n_space, n_spin, n_cons, nt, nsp, nj = layout
    slots = items.shape[0]
    nev = elementals.shape[-1]
    chunk = parts[0].shape[-2]
    unit = min(chunk, nj)
    group = math.gcd(slots, 4)
    parts = [part.reshape(n_cons * chunk // unit, unit, nev) for part in parts]
    return pl.pallas_call(
        functools.partial(contract_kernel, layout, chunk // unit, group),
        out_shape=jax.ShapeDtypeStruct((2, slots, nev, nev), jnp.bfloat16),
        in_specs=[pl.BlockSpec(memory_space=pltpu.SMEM)] * 3
        + [pl.BlockSpec(memory_space=pltpu.VMEM)]
        + [pl.BlockSpec(memory_space=pl.ANY)] * len(parts),
        out_specs=pl.BlockSpec(memory_space=pl.ANY),
        scratch_shapes=[
            pltpu.VMEM((len(parts),) + parts[0].shape, jnp.bfloat16),
            pltpu.VMEM((slots, 2, nev, nev), jnp.bfloat16),
            pltpu.VMEM((group, 2 * nev, nev), jnp.bfloat16),
            pltpu.SemaphoreType.DMA((len(parts),)),
            pltpu.SemaphoreType.DMA((slots,)),
        ],
        compiler_params=pltpu.CompilerParams(vmem_limit_bytes=32 * 2**20),
        cost_estimate=pl.CostEstimate(
            flops=16 * slots * nev**3,
            bytes_accessed=2 * (elementals.size + 2 * slots * nev * nev),
            transcendentals=0,
        ),
    )(
        pos,
        items.reshape(-1),
        live,
        pltpu.with_memory_space_constraint(elementals, pltpu.VMEM),
        *parts,
    )


def body(eigvecs, solutions, elementals, op_list, live_count):
    n_space, n_spin, n_cons = (lax.axis_size(a) for a in ("space", "spin", "cons"))
    pos = jnp.stack([lax.axis_index(a) for a in ("space", "spin", "cons")]).astype(jnp.int32)
    _, nt, nsp, nj, _ = solutions.shape
    sends = partial_taus(pos, eigvecs, solutions, n_space, jnp.bfloat16)
    space_steps, spin_steps, cons_steps = partners(n_space), partners(n_spin), partners(n_cons)
    got = [sends[0]] + [
        lax.ppermute(sends[s], "space", space_steps[s]) for s in range(1, n_space)
    ]
    mine = functools.reduce(jnp.add, [part.astype(jnp.float32) for part in got]).astype(jnp.bfloat16)
    column = jnp.stack(
        [mine] + [lax.ppermute(mine, "cons", cons_steps[s]) for s in range(1, n_cons)]
    )
    plane = [column] + [
        lax.ppermute(column, "space", space_steps[s]) for s in range(1, n_space)
    ]
    parts = list(plane)
    for s in range(1, n_spin):
        parts += [lax.ppermute(part, "spin", spin_steps[s]) for part in plane]
    layout = (n_space, n_spin, n_cons, nt, nsp, nj)
    return contract(pos, op_list[0], live_count, elementals, parts, layout)


def solution(mesh):
    return jax.shard_map(
        body,
        mesh=mesh,
        in_specs=(
            P(None, None, None, "space"),
            P(None, None, "spin", "cons", "space"),
            P(),
            P(("space", "spin", "cons"), None, None),
            P(("space", "spin", "cons")),
        ),
        out_specs=P(None, ("space", "spin", "cons"), None, None),
        check_vma=False,
    )
```

```python
import functools
import math

import jax
import jax.numpy as jnp
from jax import lax
from jax.experimental import pallas as pl
from jax.experimental.pallas import tpu as pltpu
from jax.sharding import PartitionSpec as P

NT_DOT = (((1,), (1,)), ((), ()))
NN_DOT = (((1,), (0,)), ((), ()))


dot = functools.partial(lax.dot_general, preferred_element_type=jnp.float32)


def partners(n):
    if n & (n - 1) == 0:
        return [[(i, i ^ s) for i in range(n)] for s in range(n)]
    return [[(i, (i + s) % n) for i in range(n)] for s in range(n)]


def partner(index, step, n):
    if n & (n - 1) == 0:
        return index ^ step
    return lax.rem(index - step + n, n)


def target(index, step, n):
    if n & (n - 1) == 0:
        return index ^ step
    return lax.rem(index + step, n)


def depth_cuts(depth):
    half = max(256, (depth // 2 + 255) // 256 * 256)
    return [(0, half), (half, depth)] if half < depth else [(0, depth)]


def partial_kernel(n_space, cuts, v_ref, s_ref, *rest):
    outs = rest[:n_space]
    v_buf, s_buf, acc, in_sem = rest[n_space:]
    _, nt, nev, _ = v_ref.shape
    _, _, nsp, nj, _ = s_ref.shape
    copies = []
    for t in range(nt):
        for c, (lo, hi) in enumerate(cuts):
            group = []
            for p in range(2):
                group += [
                    pltpu.make_async_copy(
                        v_ref.at[p, t, :, lo:hi], v_buf.at[p, t, :, lo:hi], in_sem.at[t, c, 2 * p]
                    ),
                    pltpu.make_async_copy(
                        s_ref.at[p, t, :, :, lo:hi],
                        s_buf.at[p, t, :, :, lo:hi],
                        in_sem.at[t, c, 2 * p + 1],
                    ),
                ]
            for copy in group:
                copy.start()
            copies.append(group)
    for t in range(nt):
        total = None
        for c, (lo, hi) in enumerate(cuts):
            for copy in copies[t * len(cuts) + c]:
                copy.wait()
            vr, vi = v_buf[0, t, :, lo:hi], v_buf[1, t, :, lo:hi]
            sr = s_buf[0, t, :, :, lo:hi].reshape(nsp * nj, hi - lo)
            si = s_buf[1, t, :, :, lo:hi].reshape(nsp * nj, hi - lo)
            both = dot(jnp.concatenate([sr, si]), vr, NT_DOT) + dot(
                jnp.concatenate([si, -sr]), vi, NT_DOT
            )
            total = both if total is None else total + both
        total = total.reshape(2, nsp, nj, nev)
        for sp in range(nsp):
            for p in range(2):
                start = ((t * nsp + sp) * 2 + p) * nj
                acc[start : start + nj, :] = total[p, sp]
    chunk = acc.shape[0] // n_space
    me = lax.axis_index("space")
    for s in range(n_space):
        first = pl.multiple_of(target(me, s, n_space) * chunk, chunk)
        outs[s][...] = acc[pl.ds(first, chunk), :].astype(outs[s].dtype)


def partial_taus(eigvecs, solutions, n_space, send_type):
    _, nt, nev, depth = eigvecs.shape
    _, _, nsp, nj, _ = solutions.shape
    rows = nt * nsp * 2 * nj
    cuts = depth_cuts(depth)
    chunk = (rows // n_space, nev)
    return pl.pallas_call(
        functools.partial(partial_kernel, n_space, cuts),
        out_shape=[pltpu.VMEM(chunk, jnp.float32)] + [pltpu.VMEM(chunk, send_type)] * (n_space - 1),
        in_specs=[pl.BlockSpec(memory_space=pl.ANY)] * 2,
        out_specs=[pl.BlockSpec(memory_space=pltpu.VMEM)] * n_space,
        scratch_shapes=[
            pltpu.VMEM(eigvecs.shape, eigvecs.dtype),
            pltpu.VMEM(solutions.shape, solutions.dtype),
            pltpu.VMEM((rows, nev), jnp.float32),
            pltpu.SemaphoreType.DMA((nt, len(cuts), 4)),
        ],
        compiler_params=pltpu.CompilerParams(vmem_limit_bytes=32 * 2**20),
        cost_estimate=pl.CostEstimate(
            flops=4 * rows * nev * depth,
            bytes_accessed=2 * (eigvecs.size + solutions.size) + 4 * rows * nev,
            transcendentals=0,
        ),
    )(
        pltpu.with_memory_space_constraint(eigvecs, pltpu.HBM),
        pltpu.with_memory_space_constraint(solutions, pltpu.HBM),
    )


def contract_kernel(layout, per_chunk, group, item_ref, live_ref, elems, *rest):
    n_space, n_spin, n_cons, nt, nsp, nj = layout
    n_parts = n_space * n_spin
    parts, out_ref = rest[:n_parts], rest[n_parts]
    tau, outs, mid, tau_sem, out_sem = rest[n_parts + 1 :]
    unit, nev = tau.shape[-2:]
    slots = out_ref.shape[1]
    scale = nev ** (-0.5)
    space, spin, cons = (lax.axis_index(a) for a in ("space", "spin", "cons"))
    loads = [pltpu.make_async_copy(part, tau.at[n], tau_sem.at[n]) for n, part in enumerate(parts)]
    for copy in loads:
        copy.start()
    for copy in loads:
        copy.wait()

    def matrix(t, a, p):
        first = ((t * nsp + a % nsp) * 2 + p) * (nj // unit)
        rows = []
        for z in range(n_cons):
            z_step = step_from(z, cons, n_cons)
            for k in range(nj // unit):
                where = first + k
                part = step_from(a // nsp, spin, n_spin) * n_space + step_from(
                    where // per_chunk, space, n_space
                )
                rows.append(tau[part, z_step * per_chunk + where % per_chunk])
        return jnp.concatenate(rows)

    def write(k):
        return pltpu.make_async_copy(outs.at[k], out_ref.at[:, k], out_sem.at[k])

    def right_half(u, item):
        e, _, b, t = item
        er, ei = elems[e, 0], elems[e, 1]
        tau_b = jnp.concatenate([matrix(t, b, 0), matrix(t, b, 1)], axis=1)
        real = dot(jnp.concatenate([er, -ei], axis=1), tau_b, NT_DOT)
        imag = dot(jnp.concatenate([ei, er], axis=1), tau_b, NT_DOT)
        mid[u, :nev] = real.astype(mid.dtype)
        mid[u, nev:] = imag.astype(mid.dtype)

    def left_half(u, k, item):
        _, a, _, t = item
        ar, ai = matrix(t, a, 0), matrix(t, a, 1)
        keep = k < live_ref[0]
        real = dot(jnp.concatenate([ar, ai], axis=1), mid[u], NN_DOT)
        imag = dot(jnp.concatenate([-ai, ar], axis=1), mid[u], NN_DOT)
        outs[k, 0] = jnp.where(keep, real * scale, 0.0).astype(outs.dtype)
        outs[k, 1] = jnp.where(keep, imag * scale, 0.0).astype(outs.dtype)

    def one_group(g, carry):
        ks = [g * group + u for u in range(group)]
        items = [tuple(item_ref[4 * k + n] for n in range(4)) for k in ks]
        right_half(0, items[0])
        for u in range(group):
            if u + 1 < group:
                right_half(u + 1, items[u + 1])
            left_half(u, ks[u], items[u])
        for k in ks:
            write(k).start()
        return carry

    def empty_group(g, carry):
        for u in range(group):
            k = g * group + u
            outs[k] = jnp.zeros(outs.shape[1:], outs.dtype)
            write(k).start()
        return carry

    n_groups = slots // group
    used = lax.div(live_ref[0] + group - 1, group)
    lax.fori_loop(0, used, one_group, 0)
    lax.fori_loop(used, n_groups, empty_group, 0)
    for k in range(slots):
        write(k).wait()


def step_from(sender, me, n):
    if n & (n - 1) == 0:
        return sender ^ me
    return lax.rem(me - sender + n, n)


def contract(items, live, elementals, parts, layout):
    n_space, n_spin, n_cons, nt, nsp, nj = layout
    slots = items.shape[0]
    nev = elementals.shape[-1]
    chunk = parts[0].shape[-2]
    unit = min(chunk, nj)
    group = math.gcd(slots, 4)
    parts = [part.reshape(n_cons * chunk // unit, unit, nev) for part in parts]
    return pl.pallas_call(
        functools.partial(contract_kernel, layout, chunk // unit, group),
        out_shape=jax.ShapeDtypeStruct((2, slots, nev, nev), jnp.bfloat16),
        in_specs=[pl.BlockSpec(memory_space=pltpu.SMEM)] * 2
        + [pl.BlockSpec(memory_space=pltpu.VMEM)] * (1 + len(parts)),
        out_specs=pl.BlockSpec(memory_space=pl.ANY),
        scratch_shapes=[
            pltpu.VMEM((len(parts),) + parts[0].shape, jnp.bfloat16),
            pltpu.VMEM((slots, 2, nev, nev), jnp.bfloat16),
            pltpu.VMEM((group, 2 * nev, nev), jnp.bfloat16),
            pltpu.SemaphoreType.DMA((len(parts),)),
            pltpu.SemaphoreType.DMA((slots,)),
        ],
        compiler_params=pltpu.CompilerParams(vmem_limit_bytes=32 * 2**20),
        cost_estimate=pl.CostEstimate(
            flops=16 * slots * nev**3,
            bytes_accessed=2 * (elementals.size + 2 * slots * nev * nev),
            transcendentals=0,
        ),
    )(
        items.reshape(-1),
        live,
        *(pltpu.with_memory_space_constraint(x, pltpu.VMEM) for x in [elementals] + parts),
    )


def body(eigvecs, solutions, elementals, op_list, live_count):
    n_space, n_spin, n_cons = (lax.axis_size(a) for a in ("space", "spin", "cons"))
    _, nt, nsp, nj, _ = solutions.shape
    sends = partial_taus(eigvecs, solutions, n_space, jnp.bfloat16)
    elementals, sends = lax.optimization_barrier((elementals, sends))
    space_steps, spin_steps, cons_steps = partners(n_space), partners(n_spin), partners(n_cons)
    got = [sends[0]] + [
        lax.ppermute(sends[s], "space", space_steps[s]) for s in range(1, n_space)
    ]
    mine = functools.reduce(jnp.add, [part.astype(jnp.float32) for part in got]).astype(jnp.bfloat16)
    column = jnp.stack(
        [mine] + [lax.ppermute(mine, "cons", cons_steps[s]) for s in range(1, n_cons)]
    )
    plane = [column] + [
        lax.ppermute(column, "space", space_steps[s]) for s in range(1, n_space)
    ]
    parts = list(plane)
    for s in range(1, n_spin):
        parts += [lax.ppermute(part, "spin", spin_steps[s]) for part in plane]
    layout = (n_space, n_spin, n_cons, nt, nsp, nj)
    return contract(op_list[0], live_count, elementals, parts, layout)


def solution(mesh):
    return jax.shard_map(
        body,
        mesh=mesh,
        in_specs=(
            P(None, None, None, "space"),
            P(None, None, "spin", "cons", "space"),
            P(),
            P(("space", "spin", "cons"), None, None),
            P(("space", "spin", "cons")),
        ),
        out_specs=P(None, ("space", "spin", "cons"), None, None),
        check_vma=False,
    )
```

```python
import functools
import math

import jax
import jax.numpy as jnp
from jax import lax
from jax.experimental import pallas as pl
from jax.experimental.pallas import tpu as pltpu
from jax.sharding import PartitionSpec as P

NT_DOT = (((1,), (1,)), ((), ()))
NN_DOT = (((1,), (0,)), ((), ()))


dot = functools.partial(lax.dot_general, preferred_element_type=jnp.float32)


def partners(n):
    if n & (n - 1) == 0:
        return [[(i, i ^ s) for i in range(n)] for s in range(n)]
    return [[(i, (i + s) % n) for i in range(n)] for s in range(n)]


def partner(index, step, n):
    if n & (n - 1) == 0:
        return index ^ step
    return lax.rem(index - step + n, n)


def target(index, step, n):
    if n & (n - 1) == 0:
        return index ^ step
    return lax.rem(index + step, n)


def depth_cuts(depth):
    half = max(256, (depth // 2 + 255) // 256 * 256)
    return [(0, half), (half, depth)] if half < depth else [(0, depth)]


def partial_kernel(n_space, also, cuts, v_ref, s_ref, *rest):
    outs = rest[:n_space]
    v_buf, s_buf, acc, in_sem = rest[n_space:]
    _, nt, nev, _ = v_ref.shape
    _, _, nsp, nj, _ = s_ref.shape
    copies = []
    for t in range(nt):
        for c, (lo, hi) in enumerate(cuts):
            group = []
            for p in range(2):
                group += [
                    pltpu.make_async_copy(
                        v_ref.at[p, t, :, lo:hi], v_buf.at[p, t, :, lo:hi], in_sem.at[t, c, 2 * p]
                    ),
                    pltpu.make_async_copy(
                        s_ref.at[p, t, :, :, lo:hi],
                        s_buf.at[p, t, :, :, lo:hi],
                        in_sem.at[t, c, 2 * p + 1],
                    ),
                ]
            for copy in group:
                copy.start()
            copies.append(group)
    for t in range(nt):
        total = None
        for c, (lo, hi) in enumerate(cuts):
            for copy in copies[t * len(cuts) + c]:
                copy.wait()
            vr, vi = v_buf[0, t, :, lo:hi], v_buf[1, t, :, lo:hi]
            sr = s_buf[0, t, :, :, lo:hi].reshape(nsp * nj, hi - lo)
            si = s_buf[1, t, :, :, lo:hi].reshape(nsp * nj, hi - lo)
            both = dot(jnp.concatenate([sr, si]), vr, NT_DOT) + dot(
                jnp.concatenate([si, -sr]), vi, NT_DOT
            )
            total = both if total is None else total + both
        total = total.reshape(2, nsp, nj, nev)
        for sp in range(nsp):
            for p in range(2):
                start = ((t * nsp + sp) * 2 + p) * nj
                acc[start : start + nj, :] = total[p, sp]
    chunk = acc.shape[0] // n_space
    me = lax.axis_index("space")
    for s in range(n_space):
        for n, step in enumerate(also):
            who = target(target(me, s, n_space), step, n_space)
            rows = acc[pl.ds(pl.multiple_of(who * chunk, chunk), chunk), :]
            outs[s][n] = rows.astype(outs[s].dtype)


def partial_taus(eigvecs, solutions, n_space, also, send_type):
    _, nt, nev, depth = eigvecs.shape
    _, _, nsp, nj, _ = solutions.shape
    rows = nt * nsp * 2 * nj
    cuts = depth_cuts(depth)
    chunk = (len(also), rows // n_space, nev)
    return pl.pallas_call(
        functools.partial(partial_kernel, n_space, also, cuts),
        out_shape=[pltpu.VMEM(chunk, jnp.float32)] + [pltpu.VMEM(chunk, send_type)] * (n_space - 1),
        in_specs=[pl.BlockSpec(memory_space=pl.ANY)] * 2,
        out_specs=[pl.BlockSpec(memory_space=pltpu.VMEM)] * n_space,
        scratch_shapes=[
            pltpu.VMEM(eigvecs.shape, eigvecs.dtype),
            pltpu.VMEM(solutions.shape, solutions.dtype),
            pltpu.VMEM((rows, nev), jnp.float32),
            pltpu.SemaphoreType.DMA((nt, len(cuts), 4)),
        ],
        compiler_params=pltpu.CompilerParams(vmem_limit_bytes=32 * 2**20),
        cost_estimate=pl.CostEstimate(
            flops=4 * rows * nev * depth,
            bytes_accessed=2 * (eigvecs.size + solutions.size) + 4 * rows * nev,
            transcendentals=0,
        ),
    )(
        pltpu.with_memory_space_constraint(eigvecs, pltpu.HBM),
        pltpu.with_memory_space_constraint(solutions, pltpu.HBM),
    )


def position(step, paired):
    return (step * 3) % 4 if paired else step


def contract_kernel(layout, firsts, per_chunk, group, item_ref, live_ref, elems, *rest):
    n_space, n_spin, n_cons, nt, nsp, nj, paired = layout
    n_parts = len(firsts)
    parts, out_ref = rest[:n_parts], rest[n_parts]
    tau, outs, mid, tau_sem, out_sem = rest[n_parts + 1 :]
    unit, nev = tau.shape[-2:]
    slots = out_ref.shape[1]
    scale = nev ** (-0.5)
    space, spin, cons = (lax.axis_index(a) for a in ("space", "spin", "cons"))
    loads = [
        pltpu.make_async_copy(part, tau.at[first : first + part.shape[0]], tau_sem.at[n])
        for n, (part, first) in enumerate(zip(parts, firsts))
    ]
    for copy in loads:
        copy.start()
    for copy in loads:
        copy.wait()

    def matrix(t, a, p):
        first = ((t * nsp + a % nsp) * 2 + p) * (nj // unit)
        rows = []
        for z in range(n_cons):
            z_step = step_from(z, cons, n_cons)
            for k in range(nj // unit):
                where = first + k
                step = step_from(where // per_chunk, space, n_space)
                part = step_from(a // nsp, spin, n_spin) * n_space + position(step, paired)
                rows.append(tau[(part * n_cons + z_step) * per_chunk + where % per_chunk])
        return jnp.concatenate(rows)

    def write(k):
        return pltpu.make_async_copy(outs.at[k], out_ref.at[:, k], out_sem.at[k])

    def right_half(u, item):
        e, _, b, t = item
        er, ei = elems[e, 0], elems[e, 1]
        tau_b = jnp.concatenate([matrix(t, b, 0), matrix(t, b, 1)], axis=1)
        real = dot(jnp.concatenate([er, -ei], axis=1), tau_b, NT_DOT)
        imag = dot(jnp.concatenate([ei, er], axis=1), tau_b, NT_DOT)
        mid[u, :nev] = real.astype(mid.dtype)
        mid[u, nev:] = imag.astype(mid.dtype)

    def left_half(u, k, item):
        _, a, _, t = item
        ar, ai = matrix(t, a, 0), matrix(t, a, 1)
        keep = k < live_ref[0]
        real = dot(jnp.concatenate([ar, ai], axis=1), mid[u], NN_DOT)
        imag = dot(jnp.concatenate([-ai, ar], axis=1), mid[u], NN_DOT)
        outs[k, 0] = jnp.where(keep, real * scale, 0.0).astype(outs.dtype)
        outs[k, 1] = jnp.where(keep, imag * scale, 0.0).astype(outs.dtype)

    def one_group(g, carry):
        ks = [g * group + u for u in range(group)]
        items = [tuple(item_ref[4 * k + n] for n in range(4)) for k in ks]
        right_half(0, items[0])
        for u in range(group):
            if u + 1 < group:
                right_half(u + 1, items[u + 1])
            left_half(u, ks[u], items[u])
            write(ks[u]).start()
        return carry

    def empty_group(g, carry):
        for u in range(group):
            k = g * group + u
            outs[k] = jnp.zeros(outs.shape[1:], outs.dtype)
            write(k).start()
        return carry

    n_groups = slots // group
    used = lax.div(live_ref[0] + group - 1, group)
    lax.fori_loop(0, used, one_group, 0)
    lax.fori_loop(used, n_groups, empty_group, 0)
    for k in range(slots):
        write(k).wait()


def step_from(sender, me, n):
    if n & (n - 1) == 0:
        return sender ^ me
    return lax.rem(me - sender + n, n)


def contract(items, live, elementals, parts, firsts, layout):
    n_space, n_spin, n_cons, nt, nsp, nj, paired = layout
    slots = items.shape[0]
    nev = elementals.shape[-1]
    chunk = nt * nsp * 2 * nj // n_space
    unit = min(chunk, nj)
    group = math.gcd(slots, 4)
    parts = [part.reshape(-1, unit, nev) for part in parts]
    firsts = [first // unit for first in firsts]
    return pl.pallas_call(
        functools.partial(contract_kernel, layout, firsts, chunk // unit, group),
        out_shape=jax.ShapeDtypeStruct((2, slots, nev, nev), jnp.bfloat16),
        in_specs=[pl.BlockSpec(memory_space=pltpu.SMEM)] * 2
        + [pl.BlockSpec(memory_space=pltpu.VMEM)] * (1 + len(parts)),
        out_specs=pl.BlockSpec(memory_space=pl.ANY),
        scratch_shapes=[
            pltpu.VMEM((n_space * n_spin * n_cons * chunk // unit, unit, nev), jnp.bfloat16),
            pltpu.VMEM((slots, 2, nev, nev), jnp.bfloat16),
            pltpu.VMEM((group, 2 * nev, nev), jnp.bfloat16),
            pltpu.SemaphoreType.DMA((len(parts),)),
            pltpu.SemaphoreType.DMA((slots,)),
        ],
        compiler_params=pltpu.CompilerParams(vmem_limit_bytes=32 * 2**20),
        cost_estimate=pl.CostEstimate(
            flops=16 * slots * nev**3,
            bytes_accessed=2 * (elementals.size + 2 * slots * nev * nev),
            transcendentals=0,
        ),
    )(
        items.reshape(-1),
        live,
        *(pltpu.with_memory_space_constraint(x, pltpu.VMEM) for x in [elementals] + parts),
    )


def body(eigvecs, solutions, elementals, op_list, live_count):
    n_space, n_spin, n_cons = (lax.axis_size(a) for a in ("space", "spin", "cons"))
    _, nt, nsp, nj, _ = solutions.shape
    paired = n_space == 4
    also = (0, n_space - 1) if paired else (0,)
    sends = partial_taus(eigvecs, solutions, n_space, also, jnp.bfloat16)
    elementals, sends = lax.optimization_barrier((elementals, sends))
    space_steps, spin_steps, cons_steps = partners(n_space), partners(n_spin), partners(n_cons)
    got = [sends[0]] + [
        lax.ppermute(sends[s], "space", space_steps[s]) for s in range(1, n_space)
    ]
    sums = functools.reduce(jnp.add, [part.astype(jnp.float32) for part in got])

    layout = (n_space, n_spin, n_cons, nt, nsp, nj, paired)

    def column(n):
        mine = sums[n].astype(jnp.bfloat16)
        return jnp.stack(
            [mine] + [lax.ppermute(mine, "cons", cons_steps[s]) for s in range(1, n_cons)]
        ).reshape(n_cons * mine.shape[0], mine.shape[1])

    own = column(0)
    rows = own.shape[0]
    held, shared = [(own, 0)], [(own, 0)]
    if paired:
        both = jnp.concatenate([own, column(1)])
        early = rows // n_cons // 2
        held = [(both, 0)]
        shared = [(sums[0, :early].astype(jnp.bfloat16), 0), (both[early:], early)]
    for s in range(1, n_space - 1 if paired else n_space):
        near = lax.ppermute(own, "space", space_steps[s])
        held.append((near, position(s, paired) * rows))
        shared.append(held[-1])
    for c in range(1, n_spin):
        for part, first in shared:
            got = lax.ppermute(part, "spin", spin_steps[c])
            held.append((got, c * n_space * rows + first))
    return contract(op_list[0], live_count, elementals, *zip(*held), layout)


def solution(mesh):
    return jax.shard_map(
        body,
        mesh=mesh,
        in_specs=(
            P(None, None, None, "space"),
            P(None, None, "spin", "cons", "space"),
            P(),
            P(("space", "spin", "cons"), None, None),
            P(("space", "spin", "cons")),
        ),
        out_specs=P(None, ("space", "spin", "cons"), None, None),
        check_vma=False,
    )
```

```python
import functools
import math

import jax
import jax.numpy as jnp
from jax import lax
from jax.experimental import pallas as pl
from jax.experimental.pallas import tpu as pltpu
from jax.sharding import PartitionSpec as P

NT_DOT = (((1,), (1,)), ((), ()))
NN_DOT = (((1,), (0,)), ((), ()))


dot = functools.partial(lax.dot_general, preferred_element_type=jnp.float32)


def partners(n):
    if n & (n - 1) == 0:
        return [[(i, i ^ s) for i in range(n)] for s in range(n)]
    return [[(i, (i + s) % n) for i in range(n)] for s in range(n)]


def partner(index, step, n):
    if n & (n - 1) == 0:
        return index ^ step
    return lax.rem(index - step + n, n)


def target(index, step, n):
    if n & (n - 1) == 0:
        return index ^ step
    return lax.rem(index + step, n)


def depth_cuts(depth):
    half = max(256, (depth // 2 + 255) // 256 * 256)
    return [(0, half), (half, depth)] if half < depth else [(0, depth)]


def partial_kernel(n_space, cuts, v_ref, s_ref, *rest):
    outs = rest[:n_space]
    v_buf, s_buf, acc, in_sem = rest[n_space:]
    _, nt, nev, _ = v_ref.shape
    _, _, nsp, nj, _ = s_ref.shape
    copies = []
    for t in range(nt):
        for c, (lo, hi) in enumerate(cuts):
            group = []
            for p in range(2):
                group += [
                    pltpu.make_async_copy(
                        v_ref.at[p, t, :, lo:hi], v_buf.at[p, t, :, lo:hi], in_sem.at[t, c, 2 * p]
                    ),
                    pltpu.make_async_copy(
                        s_ref.at[p, t, :, :, lo:hi],
                        s_buf.at[p, t, :, :, lo:hi],
                        in_sem.at[t, c, 2 * p + 1],
                    ),
                ]
            for copy in group:
                copy.start()
            copies.append(group)
    for t in range(nt):
        total = None
        for c, (lo, hi) in enumerate(cuts):
            for copy in copies[t * len(cuts) + c]:
                copy.wait()
            vr, vi = v_buf[0, t, :, lo:hi], v_buf[1, t, :, lo:hi]
            sr = s_buf[0, t, :, :, lo:hi].reshape(nsp * nj, hi - lo)
            si = s_buf[1, t, :, :, lo:hi].reshape(nsp * nj, hi - lo)
            both = dot(jnp.concatenate([sr, si]), vr, NT_DOT) + dot(
                jnp.concatenate([si, -sr]), vi, NT_DOT
            )
            total = both if total is None else total + both
        total = total.reshape(2, nsp, nj, nev)
        for sp in range(nsp):
            for p in range(2):
                start = ((t * nsp + sp) * 2 + p) * nj
                acc[start : start + nj, :] = total[p, sp]
    chunk = acc.shape[0] // n_space
    me = lax.axis_index("space")
    for s in range(n_space):
        rows = pl.ds(pl.multiple_of(target(me, s, n_space) * chunk, chunk), chunk)
        outs[s][...] = acc[rows, :].astype(outs[s].dtype)


def partial_taus(eigvecs, solutions, n_space, send_type):
    _, nt, nev, depth = eigvecs.shape
    _, _, nsp, nj, _ = solutions.shape
    rows = nt * nsp * 2 * nj
    cuts = depth_cuts(depth)
    chunk = (rows // n_space, nev)
    return pl.pallas_call(
        functools.partial(partial_kernel, n_space, cuts),
        out_shape=[pltpu.VMEM(chunk, jnp.float32)] + [pltpu.VMEM(chunk, send_type)] * (n_space - 1),
        in_specs=[pl.BlockSpec(memory_space=pl.ANY)] * 2,
        out_specs=[pl.BlockSpec(memory_space=pltpu.VMEM)] * n_space,
        scratch_shapes=[
            pltpu.VMEM(eigvecs.shape, eigvecs.dtype),
            pltpu.VMEM(solutions.shape, solutions.dtype),
            pltpu.VMEM((rows, nev), jnp.float32),
            pltpu.SemaphoreType.DMA((nt, len(cuts), 4)),
        ],
        compiler_params=pltpu.CompilerParams(vmem_limit_bytes=32 * 2**20),
        cost_estimate=pl.CostEstimate(
            flops=4 * rows * nev * depth,
            bytes_accessed=2 * (eigvecs.size + solutions.size) + 4 * rows * nev,
            transcendentals=0,
        ),
    )(
        pltpu.with_memory_space_constraint(eigvecs, pltpu.HBM),
        pltpu.with_memory_space_constraint(solutions, pltpu.HBM),
    )


def contract_kernel(layout, firsts, per_chunk, group, item_in, live_in, elems, *rest):
    n_space, n_spin, n_cons, nt, nsp, nj = layout
    n_parts = len(firsts)
    parts, out_ref = rest[:n_parts], rest[n_parts]
    tau, outs, mid, item_ref, live_ref, out_sem, slot_sem = rest[n_parts + 1 :]
    unit, nev = tau.shape[-2:]
    slots = out_ref.shape[1]
    scale = nev ** (-0.5)
    space, spin, cons = (lax.axis_index(a) for a in ("space", "spin", "cons"))
    loads = [
        pltpu.make_async_copy(item_in, item_ref, slot_sem.at[0]),
        pltpu.make_async_copy(live_in, live_ref, slot_sem.at[1]),
    ]
    for copy in loads:
        copy.start()
    for part, first in zip(parts, firsts):
        tau[first : first + part.shape[0]] = part[...]
    for copy in loads:
        copy.wait()

    def matrix(t, a, p):
        first = ((t * nsp + a % nsp) * 2 + p) * (nj // unit)
        rows = []
        for z in range(n_cons):
            z_step = step_from(z, cons, n_cons)
            for k in range(nj // unit):
                where = first + k
                step = step_from(where // per_chunk, space, n_space)
                part = step_from(a // nsp, spin, n_spin) * n_space + step
                rows.append(tau[(part * n_cons + z_step) * per_chunk + where % per_chunk])
        return jnp.concatenate(rows)

    def write(k):
        return pltpu.make_async_copy(outs.at[k], out_ref.at[:, k], out_sem.at[k])

    def right_half(u, item):
        e, _, b, t = item
        er, ei = elems[e, 0], elems[e, 1]
        tau_b = jnp.concatenate([matrix(t, b, 0), matrix(t, b, 1)], axis=1)
        real = dot(jnp.concatenate([er, -ei], axis=1), tau_b, NT_DOT)
        imag = dot(jnp.concatenate([ei, er], axis=1), tau_b, NT_DOT)
        mid[u, :nev] = real.astype(mid.dtype)
        mid[u, nev:] = imag.astype(mid.dtype)

    def left_half(u, k, item):
        _, a, _, t = item
        ar, ai = matrix(t, a, 0), matrix(t, a, 1)
        keep = k < live_ref[0]
        real = dot(jnp.concatenate([ar, ai], axis=1), mid[u], NN_DOT)
        imag = dot(jnp.concatenate([-ai, ar], axis=1), mid[u], NN_DOT)
        outs[k, 0] = jnp.where(keep, real * scale, 0.0).astype(outs.dtype)
        outs[k, 1] = jnp.where(keep, imag * scale, 0.0).astype(outs.dtype)

    def one_group(g, carry):
        ks = [g * group + u for u in range(group)]
        items = [tuple(item_ref[n, k] for n in range(4)) for k in ks]
        right_half(0, items[0])
        for u in range(group):
            if u + 1 < group:
                right_half(u + 1, items[u + 1])
            left_half(u, ks[u], items[u])
            write(ks[u]).start()
        return carry

    def empty_group(g, carry):
        for u in range(group):
            k = g * group + u
            outs[k] = jnp.zeros(outs.shape[1:], outs.dtype)
            write(k).start()
        return carry

    n_groups = slots // group
    used = lax.div(live_ref[0] + group - 1, group)
    lax.fori_loop(0, used, one_group, 0)
    lax.fori_loop(used, n_groups, empty_group, 0)
    for k in range(slots):
        write(k).wait()


def step_from(sender, me, n):
    if n & (n - 1) == 0:
        return sender ^ me
    return lax.rem(me - sender + n, n)


def contract(items, live, elementals, parts, firsts, layout):
    n_space, n_spin, n_cons, nt, nsp, nj = layout
    slots = items.shape[1]
    nev = elementals.shape[-1]
    chunk = nt * nsp * 2 * nj // n_space
    unit = min(chunk, nj)
    group = math.gcd(slots, 4)
    parts = [part.reshape(-1, unit, nev) for part in parts]
    firsts = [first // unit for first in firsts]
    return pl.pallas_call(
        functools.partial(contract_kernel, layout, firsts, chunk // unit, group),
        out_shape=jax.ShapeDtypeStruct((2, slots, nev, nev), jnp.bfloat16),
        in_specs=[pl.BlockSpec(memory_space=pl.ANY)] * 2
        + [pl.BlockSpec(memory_space=pltpu.VMEM)] * (1 + len(parts)),
        out_specs=pl.BlockSpec(memory_space=pl.ANY),
        scratch_shapes=[
            pltpu.VMEM((n_space * n_spin * n_cons * chunk // unit, unit, nev), jnp.bfloat16),
            pltpu.VMEM((slots, 2, nev, nev), jnp.bfloat16),
            pltpu.VMEM((group, 2 * nev, nev), jnp.bfloat16),
            pltpu.SMEM(items.shape, jnp.int32),
            pltpu.SMEM(live.shape, jnp.int32),
            pltpu.SemaphoreType.DMA((slots,)),
            pltpu.SemaphoreType.DMA((2,)),
        ],
        compiler_params=pltpu.CompilerParams(vmem_limit_bytes=32 * 2**20),
        cost_estimate=pl.CostEstimate(
            flops=16 * slots * nev**3,
            bytes_accessed=2 * (elementals.size + 2 * slots * nev * nev),
            transcendentals=0,
        ),
    )(
        items,
        live,
        *(pltpu.with_memory_space_constraint(x, pltpu.VMEM) for x in [elementals] + parts),
    )


def body(eigvecs, solutions, elementals, op_list, live_count):
    n_space, n_spin, n_cons = (lax.axis_size(a) for a in ("space", "spin", "cons"))
    _, nt, nev, _ = eigvecs.shape
    _, _, nsp, nj, _ = solutions.shape
    sends = partial_taus(eigvecs, solutions, n_space, jnp.bfloat16)
    elementals, sends = lax.optimization_barrier((elementals, sends))
    space_steps, spin_steps, cons_steps = partners(n_space), partners(n_spin), partners(n_cons)

    def over_space(x, s):
        return lax.ppermute(x, "space", space_steps[s])

    def over_cons(x, s):
        return lax.ppermute(x, "cons", cons_steps[s])

    got = [sends[0]] + [over_space(sends[s], s) for s in range(1, n_space)]
    mine = functools.reduce(jnp.add, [part.astype(jnp.float32) for part in got])
    mine = mine.astype(jnp.bfloat16)
    pieces = [mine] + [over_cons(mine, s) for s in range(1, n_cons)]
    own = jnp.stack(pieces).reshape(-1, nev)
    rows = own.shape[0]

    far = []
    if n_space == 4:
        across = n_space - 1
        first = over_space(mine, across)
        own, first = lax.optimization_barrier((own, first))
        rest = [over_cons(first, 1)] + [over_space(pieces[s], across) for s in range(2, n_cons)]
        place = across * rows
        far = [(first, place), (jnp.stack(rest).reshape(-1, nev), place + mine.shape[0])]
    near = range(1, n_space - 1 if far else n_space)
    held = [(own, 0)] + far + [(over_space(own, s), s * rows) for s in near]
    for c in range(1, n_spin):
        held += [
            (lax.ppermute(part, "spin", spin_steps[c]), c * n_space * rows + place)
            for part, place in held[: len(far) + len(near) + 1]
        ]
    layout = (n_space, n_spin, n_cons, nt, nsp, nj)
    return contract(op_list[0].T, live_count, elementals, *zip(*held), layout)


def solution(mesh):
    return jax.shard_map(
        body,
        mesh=mesh,
        in_specs=(
            P(None, None, None, "space"),
            P(None, None, "spin", "cons", "space"),
            P(),
            P(("space", "spin", "cons"), None, None),
            P(("space", "spin", "cons")),
        ),
        out_specs=P(None, ("space", "spin", "cons"), None, None),
        check_vma=False,
    )
```

```python
import functools
import math

import jax
import jax.numpy as jnp
from jax import lax
from jax.experimental import pallas as pl
from jax.experimental.pallas import tpu as pltpu
from jax.sharding import PartitionSpec as P

NT_DOT = (((1,), (1,)), ((), ()))
NN_DOT = (((1,), (0,)), ((), ()))


dot = functools.partial(lax.dot_general, preferred_element_type=jnp.float32)


def partners(n):
    if n & (n - 1) == 0:
        return [[(i, i ^ s) for i in range(n)] for s in range(n)]
    return [[(i, (i + s) % n) for i in range(n)] for s in range(n)]


def partner(index, step, n):
    if n & (n - 1) == 0:
        return index ^ step
    return lax.rem(index - step + n, n)


def target(index, step, n):
    if n & (n - 1) == 0:
        return index ^ step
    return lax.rem(index + step, n)


def depth_cuts(depth):
    half = max(256, (depth // 2 + 255) // 256 * 256)
    return [(0, half), (half, depth)] if half < depth else [(0, depth)]


def partial_kernel(n_space, cuts, v_ref, s_ref, *rest):
    outs = rest[:n_space]
    v_buf, s_buf, acc, in_sem = rest[n_space:]
    _, nt, nev, _ = v_ref.shape
    _, _, nsp, nj, _ = s_ref.shape
    copies = []
    for t in range(nt):
        for c, (lo, hi) in enumerate(cuts):
            group = []
            for p in range(2):
                group += [
                    pltpu.make_async_copy(
                        v_ref.at[p, t, :, lo:hi], v_buf.at[p, t, :, lo:hi], in_sem.at[t, c, 2 * p]
                    ),
                    pltpu.make_async_copy(
                        s_ref.at[p, t, :, :, lo:hi],
                        s_buf.at[p, t, :, :, lo:hi],
                        in_sem.at[t, c, 2 * p + 1],
                    ),
                ]
            for copy in group:
                copy.start()
            copies.append(group)
    for t in range(nt):
        total = None
        for c, (lo, hi) in enumerate(cuts):
            for copy in copies[t * len(cuts) + c]:
                copy.wait()
            vr, vi = v_buf[0, t, :, lo:hi], v_buf[1, t, :, lo:hi]
            sr = s_buf[0, t, :, :, lo:hi].reshape(nsp * nj, hi - lo)
            si = s_buf[1, t, :, :, lo:hi].reshape(nsp * nj, hi - lo)
            both = dot(jnp.concatenate([sr, si]), vr, NT_DOT) + dot(
                jnp.concatenate([si, -sr]), vi, NT_DOT
            )
            total = both if total is None else total + both
        total = total.reshape(2, nsp, nj, nev)
        for sp in range(nsp):
            for p in range(2):
                start = ((t * nsp + sp) * 2 + p) * nj
                acc[start : start + nj, :] = total[p, sp]
    chunk = acc.shape[0] // n_space
    me = lax.axis_index("space")
    for s in range(n_space):
        rows = pl.ds(pl.multiple_of(target(me, s, n_space) * chunk, chunk), chunk)
        outs[s][...] = acc[rows, :].astype(outs[s].dtype)


def partial_taus(eigvecs, solutions, n_space, send_type):
    _, nt, nev, depth = eigvecs.shape
    _, _, nsp, nj, _ = solutions.shape
    rows = nt * nsp * 2 * nj
    cuts = depth_cuts(depth)
    chunk = (rows // n_space, nev)
    return pl.pallas_call(
        functools.partial(partial_kernel, n_space, cuts),
        out_shape=[pltpu.VMEM(chunk, jnp.float32)] + [pltpu.VMEM(chunk, send_type)] * (n_space - 1),
        in_specs=[pl.BlockSpec(memory_space=pl.ANY)] * 2,
        out_specs=[pl.BlockSpec(memory_space=pltpu.VMEM)] * n_space,
        scratch_shapes=[
            pltpu.VMEM(eigvecs.shape, eigvecs.dtype),
            pltpu.VMEM(solutions.shape, solutions.dtype),
            pltpu.VMEM((rows, nev), jnp.float32),
            pltpu.SemaphoreType.DMA((nt, len(cuts), 4)),
        ],
        compiler_params=pltpu.CompilerParams(vmem_limit_bytes=32 * 2**20),
        cost_estimate=pl.CostEstimate(
            flops=4 * rows * nev * depth,
            bytes_accessed=2 * (eigvecs.size + solutions.size) + 4 * rows * nev,
            transcendentals=0,
        ),
    )(
        pltpu.with_memory_space_constraint(eigvecs, pltpu.HBM),
        pltpu.with_memory_space_constraint(solutions, pltpu.HBM),
    )


def contract_kernel(layout, firsts, per_chunk, group, item_in, live_in, elems, *rest):
    n_space, n_spin, n_cons, nt, nsp, nj = layout
    n_parts = len(firsts)
    parts, out_ref = rest[:n_parts], rest[n_parts]
    tau, outs, mid, item_ref, live_ref, out_sem, slot_sem = rest[n_parts + 1 :]
    unit, nev = tau.shape[-2:]
    slots = out_ref.shape[1]
    scale = nev ** (-0.5)
    space, spin, cons = (lax.axis_index(a) for a in ("space", "spin", "cons"))
    loads = [
        pltpu.make_async_copy(item_in, item_ref, slot_sem.at[0]),
        pltpu.make_async_copy(live_in, live_ref, slot_sem.at[1]),
    ]
    for copy in loads:
        copy.start()
    for part, first in zip(parts, firsts):
        tau[first : first + part.shape[0]] = part[...]
    for copy in loads:
        copy.wait()

    def matrix(t, a, p):
        first = ((t * nsp + a % nsp) * 2 + p) * (nj // unit)
        rows = []
        for z in range(n_cons):
            z_step = step_from(z, cons, n_cons)
            for k in range(nj // unit):
                where = first + k
                step = step_from(where // per_chunk, space, n_space)
                part = step_from(a // nsp, spin, n_spin) * n_space + step
                rows.append(tau[(part * n_cons + z_step) * per_chunk + where % per_chunk])
        return jnp.concatenate(rows)

    def write(k):
        return pltpu.make_async_copy(outs.at[k], out_ref.at[:, k], out_sem.at[k])

    def right_half(u, item):
        e, _, b, t = item
        er, ei = elems[e, 0], elems[e, 1]
        tau_b = jnp.concatenate([matrix(t, b, 0), matrix(t, b, 1)], axis=1)
        real = dot(jnp.concatenate([er, -ei], axis=1), tau_b, NT_DOT)
        imag = dot(jnp.concatenate([ei, er], axis=1), tau_b, NT_DOT)
        mid[u, :nev] = real.astype(mid.dtype)
        mid[u, nev:] = imag.astype(mid.dtype)

    def left_half(u, k, item):
        _, a, _, t = item
        ar, ai = matrix(t, a, 0), matrix(t, a, 1)
        keep = k < live_ref[0]
        real = dot(jnp.concatenate([ar, ai], axis=1), mid[u], NN_DOT)
        imag = dot(jnp.concatenate([-ai, ar], axis=1), mid[u], NN_DOT)
        outs[k, 0] = jnp.where(keep, real * scale, 0.0).astype(outs.dtype)
        outs[k, 1] = jnp.where(keep, imag * scale, 0.0).astype(outs.dtype)

    def one_group(g, carry):
        ks = [g * group + u for u in range(group)]
        items = [tuple(item_ref[n, k] for n in range(4)) for k in ks]
        right_half(0, items[0])
        for u in range(group):
            if u + 1 < group:
                right_half(u + 1, items[u + 1])
            left_half(u, ks[u], items[u])
            write(ks[u]).start()
        return carry

    def empty_group(g, carry):
        for u in range(group):
            k = g * group + u
            outs[k] = jnp.zeros(outs.shape[1:], outs.dtype)
            write(k).start()
        return carry

    n_groups = slots // group
    used = lax.div(live_ref[0] + group - 1, group)
    lax.fori_loop(0, used, one_group, 0)
    lax.fori_loop(used, n_groups, empty_group, 0)
    for k in range(slots):
        write(k).wait()


def step_from(sender, me, n):
    if n & (n - 1) == 0:
        return sender ^ me
    return lax.rem(me - sender + n, n)


def contract(items, live, elementals, parts, firsts, layout):
    n_space, n_spin, n_cons, nt, nsp, nj = layout
    slots = items.shape[1]
    nev = elementals.shape[-1]
    chunk = nt * nsp * 2 * nj // n_space
    unit = min(chunk, nj)
    group = math.gcd(slots, 4)
    parts = [part.reshape(-1, unit, nev) for part in parts]
    firsts = [first // unit for first in firsts]
    return pl.pallas_call(
        functools.partial(contract_kernel, layout, firsts, chunk // unit, group),
        out_shape=jax.ShapeDtypeStruct((2, slots, nev, nev), jnp.bfloat16),
        in_specs=[pl.BlockSpec(memory_space=pl.ANY)] * 2
        + [pl.BlockSpec(memory_space=pltpu.VMEM)] * (1 + len(parts)),
        out_specs=pl.BlockSpec(memory_space=pl.ANY),
        scratch_shapes=[
            pltpu.VMEM((n_space * n_spin * n_cons * chunk // unit, unit, nev), jnp.bfloat16),
            pltpu.VMEM((slots, 2, nev, nev), jnp.bfloat16),
            pltpu.VMEM((group, 2 * nev, nev), jnp.bfloat16),
            pltpu.SMEM(items.shape, jnp.int32),
            pltpu.SMEM(live.shape, jnp.int32),
            pltpu.SemaphoreType.DMA((slots,)),
            pltpu.SemaphoreType.DMA((2,)),
        ],
        compiler_params=pltpu.CompilerParams(vmem_limit_bytes=32 * 2**20),
        cost_estimate=pl.CostEstimate(
            flops=16 * slots * nev**3,
            bytes_accessed=2 * (elementals.size + 2 * slots * nev * nev),
            transcendentals=0,
        ),
    )(
        items,
        live,
        *(pltpu.with_memory_space_constraint(x, pltpu.VMEM) for x in [elementals] + parts),
    )


def body(eigvecs, solutions, elementals, op_list, live_count):
    n_space, n_spin, n_cons = (lax.axis_size(a) for a in ("space", "spin", "cons"))
    _, nt, nev, _ = eigvecs.shape
    _, _, nsp, nj, _ = solutions.shape
    sends = partial_taus(eigvecs, solutions, n_space, jnp.bfloat16)
    elementals, sends = lax.optimization_barrier((elementals, sends))
    space_steps, spin_steps, cons_steps = partners(n_space), partners(n_spin), partners(n_cons)

    def over_space(x, s):
        return lax.ppermute(x, "space", space_steps[s])

    def over_cons(x, s):
        return lax.ppermute(x, "cons", cons_steps[s])

    got = [sends[0]] + [over_space(sends[s], s) for s in range(1, n_space)[::-1]]
    mine = functools.reduce(jnp.add, [part.astype(jnp.float32) for part in got])
    mine = mine.astype(jnp.bfloat16)
    pieces = [mine] + [over_cons(mine, s) for s in range(1, n_cons)]
    own = jnp.stack(pieces).reshape(-1, nev)
    rows = own.shape[0]

    far = []
    if n_space == 4:
        across = n_space - 1
        first = over_space(mine, across)
        own, first = lax.optimization_barrier((own, first))
        place = across * rows
        height = mine.shape[0]
        rest = over_space(jnp.stack(pieces[2:]).reshape(-1, nev), across)
        far = [(jnp.stack([first, over_cons(first, 1)]).reshape(-1, nev), place), (rest, place + 2 * height)]
    near = range(1, n_space - 1 if far else n_space)
    held = [(own, 0)] + far + [(over_space(own, s), s * rows) for s in near]
    for c in range(1, n_spin):
        held += [
            (lax.ppermute(part, "spin", spin_steps[c]), c * n_space * rows + place)
            for part, place in held[: len(far) + len(near) + 1]
        ]
    layout = (n_space, n_spin, n_cons, nt, nsp, nj)
    return contract(op_list[0].T, live_count, elementals, *zip(*held), layout)


def solution(mesh):
    return jax.shard_map(
        body,
        mesh=mesh,
        in_specs=(
            P(None, None, None, "space"),
            P(None, None, "spin", "cons", "space"),
            P(),
            P(("space", "spin", "cons"), None, None),
            P(("space", "spin", "cons")),
        ),
        out_specs=P(None, ("space", "spin", "cons"), None, None),
        check_vma=False,
    )
```

```python
import functools
import math

import jax
import jax.numpy as jnp
from jax import lax
from jax.experimental import pallas as pl
from jax.experimental.pallas import tpu as pltpu
from jax.sharding import PartitionSpec as P

NT_DOT = (((1,), (1,)), ((), ()))
NN_DOT = (((1,), (0,)), ((), ()))


dot = functools.partial(lax.dot_general, preferred_element_type=jnp.float32)


def partners(n):
    if n & (n - 1) == 0:
        return [[(i, i ^ s) for i in range(n)] for s in range(n)]
    return [[(i, (i + s) % n) for i in range(n)] for s in range(n)]


def partner(index, step, n):
    if n & (n - 1) == 0:
        return index ^ step
    return lax.rem(index - step + n, n)


def target(index, step, n):
    if n & (n - 1) == 0:
        return index ^ step
    return lax.rem(index + step, n)


def depth_cuts(depth):
    half = max(256, (depth // 2 + 255) // 256 * 256)
    return [(0, half), (half, depth)] if half < depth else [(0, depth)]


def partial_kernel(n_space, cuts, v_ref, s_ref, *rest):
    outs = rest[:n_space]
    v_buf, s_buf, acc, in_sem = rest[n_space:]
    _, nt, nev, _ = v_ref.shape
    _, _, nsp, nj, _ = s_ref.shape
    copies = []
    for t in range(nt):
        for c, (lo, hi) in enumerate(cuts):
            group = []
            for p in range(2):
                group += [
                    pltpu.make_async_copy(
                        v_ref.at[p, t, :, lo:hi], v_buf.at[p, t, :, lo:hi], in_sem.at[t, c, 2 * p]
                    ),
                    pltpu.make_async_copy(
                        s_ref.at[p, t, :, :, lo:hi],
                        s_buf.at[p, t, :, :, lo:hi],
                        in_sem.at[t, c, 2 * p + 1],
                    ),
                ]
            for copy in group:
                copy.start()
            copies.append(group)
    for t in range(nt):
        total = None
        for c, (lo, hi) in enumerate(cuts):
            for copy in copies[t * len(cuts) + c]:
                copy.wait()
            vr, vi = v_buf[0, t, :, lo:hi], v_buf[1, t, :, lo:hi]
            sr = s_buf[0, t, :, :, lo:hi].reshape(nsp * nj, hi - lo)
            si = s_buf[1, t, :, :, lo:hi].reshape(nsp * nj, hi - lo)
            both = dot(jnp.concatenate([sr, si]), vr, NT_DOT) + dot(
                jnp.concatenate([si, -sr]), vi, NT_DOT
            )
            total = both if total is None else total + both
        total = total.reshape(2, nsp, nj, nev)
        for sp in range(nsp):
            for p in range(2):
                start = ((t * nsp + sp) * 2 + p) * nj
                acc[start : start + nj, :] = total[p, sp]
    chunk = acc.shape[0] // n_space
    me = lax.axis_index("space")
    for s in range(n_space):
        rows = pl.ds(pl.multiple_of(target(me, s, n_space) * chunk, chunk), chunk)
        outs[s][...] = acc[rows, :].astype(outs[s].dtype)


def partial_taus(eigvecs, solutions, n_space, send_type):
    _, nt, nev, depth = eigvecs.shape
    _, _, nsp, nj, _ = solutions.shape
    rows = nt * nsp * 2 * nj
    cuts = depth_cuts(depth)
    chunk = (rows // n_space, nev)
    return pl.pallas_call(
        functools.partial(partial_kernel, n_space, cuts),
        out_shape=[pltpu.VMEM(chunk, jnp.float32)] + [pltpu.VMEM(chunk, send_type)] * (n_space - 1),
        in_specs=[pl.BlockSpec(memory_space=pl.ANY)] * 2,
        out_specs=[pl.BlockSpec(memory_space=pltpu.VMEM)] * n_space,
        scratch_shapes=[
            pltpu.VMEM(eigvecs.shape, eigvecs.dtype),
            pltpu.VMEM(solutions.shape, solutions.dtype),
            pltpu.VMEM((rows, nev), jnp.float32),
            pltpu.SemaphoreType.DMA((nt, len(cuts), 4)),
        ],
        compiler_params=pltpu.CompilerParams(vmem_limit_bytes=32 * 2**20),
        cost_estimate=pl.CostEstimate(
            flops=4 * rows * nev * depth,
            bytes_accessed=2 * (eigvecs.size + solutions.size) + 4 * rows * nev,
            transcendentals=0,
        ),
    )(
        pltpu.with_memory_space_constraint(eigvecs, pltpu.HBM),
        pltpu.with_memory_space_constraint(solutions, pltpu.HBM),
    )


def contract_kernel(layout, firsts, per_chunk, group, item_in, live_in, elems, *rest):
    n_space, n_spin, n_cons, nt, nsp, nj = layout
    n_parts = len(firsts)
    parts, out_ref = rest[:n_parts], rest[n_parts]
    tau, outs, mid, item_ref, live_ref, out_sem, slot_sem = rest[n_parts + 1 :]
    unit, nev = tau.shape[-2:]
    slots = out_ref.shape[1]
    scale = nev ** (-0.5)
    space, spin, cons = (lax.axis_index(a) for a in ("space", "spin", "cons"))
    loads = [
        pltpu.make_async_copy(item_in, item_ref, slot_sem.at[0]),
        pltpu.make_async_copy(live_in, live_ref, slot_sem.at[1]),
    ]
    for copy in loads:
        copy.start()
    for part, first in zip(parts, firsts):
        tau[first : first + part.shape[0]] = part[...]
    for copy in loads:
        copy.wait()

    def matrix(t, a, p):
        first = ((t * nsp + a % nsp) * 2 + p) * (nj // unit)
        rows = []
        for z in range(n_cons):
            z_step = step_from(z, cons, n_cons)
            for k in range(nj // unit):
                where = first + k
                step = step_from(where // per_chunk, space, n_space)
                part = step_from(a // nsp, spin, n_spin) * n_space + step
                rows.append(tau[(part * n_cons + z_step) * per_chunk + where % per_chunk])
        return jnp.concatenate(rows)

    def write(k):
        return pltpu.make_async_copy(outs.at[k], out_ref.at[:, k], out_sem.at[k])

    def right_half(u, item):
        e, _, b, t = item
        er, ei = elems[e, 0], elems[e, 1]
        tau_b = jnp.concatenate([matrix(t, b, 0), matrix(t, b, 1)], axis=1)
        real = dot(jnp.concatenate([er, -ei], axis=1), tau_b, NT_DOT)
        imag = dot(jnp.concatenate([ei, er], axis=1), tau_b, NT_DOT)
        mid[u, :nev] = real.astype(mid.dtype)
        mid[u, nev:] = imag.astype(mid.dtype)

    def left_half(u, k, item):
        _, a, _, t = item
        ar, ai = matrix(t, a, 0), matrix(t, a, 1)
        keep = k < live_ref[0]
        real = dot(jnp.concatenate([ar, ai], axis=1), mid[u], NN_DOT)
        imag = dot(jnp.concatenate([-ai, ar], axis=1), mid[u], NN_DOT)
        outs[k, 0] = jnp.where(keep, real * scale, 0.0).astype(outs.dtype)
        outs[k, 1] = jnp.where(keep, imag * scale, 0.0).astype(outs.dtype)

    def slots_from(first, size):
        ks = [first + u for u in range(size)]
        items = [tuple(item_ref[n, k] for n in range(4)) for k in ks]
        right_half(0, items[0])
        for u in range(size):
            if u + 1 < size:
                right_half(u + 1, items[u + 1])
            left_half(u, ks[u], items[u])
            write(ks[u]).start()

    def empty(k, carry):
        outs[k] = jnp.zeros(outs.shape[1:], outs.dtype)
        write(k).start()
        return carry

    def large(g, carry):
        slots_from(g * 2 * group, 2 * group)
        return carry

    def small(g, carry):
        slots_from(g * group, group)
        return carry

    pairs = lax.div(live_ref[0], 2 * group)
    used = lax.div(live_ref[0] + group - 1, group)
    lax.fori_loop(used * group, slots, empty, 0)
    lax.fori_loop(0, pairs, large, 0)
    lax.fori_loop(2 * pairs, used, small, 0)
    for k in range(slots):
        write(k).wait()


def step_from(sender, me, n):
    if n & (n - 1) == 0:
        return sender ^ me
    return lax.rem(me - sender + n, n)


def contract(items, live, elementals, parts, firsts, layout):
    n_space, n_spin, n_cons, nt, nsp, nj = layout
    slots = items.shape[1]
    nev = elementals.shape[-1]
    chunk = nt * nsp * 2 * nj // n_space
    unit = min(chunk, nj)
    group = math.gcd(slots, 4)
    parts = [part.reshape(-1, unit, nev) for part in parts]
    firsts = [first // unit for first in firsts]
    return pl.pallas_call(
        functools.partial(contract_kernel, layout, firsts, chunk // unit, group),
        out_shape=jax.ShapeDtypeStruct((2, slots, nev, nev), jnp.bfloat16),
        in_specs=[pl.BlockSpec(memory_space=pl.ANY)] * 2
        + [pl.BlockSpec(memory_space=pltpu.VMEM)] * (1 + len(parts)),
        out_specs=pl.BlockSpec(memory_space=pl.ANY),
        scratch_shapes=[
            pltpu.VMEM((n_space * n_spin * n_cons * chunk // unit, unit, nev), jnp.bfloat16),
            pltpu.VMEM((slots, 2, nev, nev), jnp.bfloat16),
            pltpu.VMEM((2 * group, 2 * nev, nev), jnp.bfloat16),
            pltpu.SMEM(items.shape, jnp.int32),
            pltpu.SMEM(live.shape, jnp.int32),
            pltpu.SemaphoreType.DMA((slots,)),
            pltpu.SemaphoreType.DMA((2,)),
        ],
        compiler_params=pltpu.CompilerParams(vmem_limit_bytes=32 * 2**20),
        cost_estimate=pl.CostEstimate(
            flops=16 * slots * nev**3,
            bytes_accessed=2 * (elementals.size + 2 * slots * nev * nev),
            transcendentals=0,
        ),
    )(
        items,
        live,
        *(pltpu.with_memory_space_constraint(x, pltpu.VMEM) for x in [elementals] + parts),
    )


def body(eigvecs, solutions, elementals, op_list, live_count):
    n_space, n_spin, n_cons = (lax.axis_size(a) for a in ("space", "spin", "cons"))
    _, nt, nev, _ = eigvecs.shape
    _, _, nsp, nj, _ = solutions.shape
    sends = partial_taus(eigvecs, solutions, n_space, jnp.bfloat16)
    elementals, sends = lax.optimization_barrier((elementals, sends))
    space_steps, spin_steps, cons_steps = partners(n_space), partners(n_spin), partners(n_cons)

    def over_space(x, s):
        return lax.ppermute(x, "space", space_steps[s])

    def over_cons(x, s):
        return lax.ppermute(x, "cons", cons_steps[s])

    got = [sends[0]] + [over_space(sends[s], s) for s in range(1, n_space)[::-1]]
    mine = functools.reduce(jnp.add, [part.astype(jnp.float32) for part in got])
    mine = mine.astype(jnp.bfloat16)
    pieces = [mine] + [over_cons(mine, s) for s in range(1, n_cons)]
    own = jnp.stack(pieces).reshape(-1, nev)
    rows = own.shape[0]

    far = []
    if n_space == 4:
        across = n_space - 1
        first = over_space(mine, across)
        own, first = lax.optimization_barrier((own, first))
        place = across * rows
        height = mine.shape[0]
        rest = over_space(jnp.stack(pieces[2:]).reshape(-1, nev), across)
        far = [(jnp.stack([first, over_cons(first, 1)]).reshape(-1, nev), place), (rest, place + 2 * height)]
    near = range(1, n_space - 1 if far else n_space)
    held = [(own, 0)] + far + [(over_space(own, s), s * rows) for s in near]
    for c in range(1, n_spin):
        held += [
            (lax.ppermute(part, "spin", spin_steps[c]), c * n_space * rows + place)
            for part, place in held[: len(far) + len(near) + 1]
        ]
    layout = (n_space, n_spin, n_cons, nt, nsp, nj)
    return contract(op_list[0].T, live_count, elementals, *zip(*held), layout)


def solution(mesh):
    return jax.shard_map(
        body,
        mesh=mesh,
        in_specs=(
            P(None, None, None, "space"),
            P(None, None, "spin", "cons", "space"),
            P(),
            P(("space", "spin", "cons"), None, None),
            P(("space", "spin", "cons")),
        ),
        out_specs=P(None, ("space", "spin", "cons"), None, None),
        check_vma=False,
    )
```

```python
import functools
import math

import jax
import jax.numpy as jnp
from jax import lax
from jax.experimental import pallas as pl
from jax.experimental.pallas import tpu as pltpu
from jax.sharding import PartitionSpec as P

NT_DOT = (((1,), (1,)), ((), ()))
NN_DOT = (((1,), (0,)), ((), ()))


dot = functools.partial(lax.dot_general, preferred_element_type=jnp.float32)


def partners(n):
    if n & (n - 1) == 0:
        return [[(i, i ^ s) for i in range(n)] for s in range(n)]
    return [[(i, (i + s) % n) for i in range(n)] for s in range(n)]


def partner(index, step, n):
    if n & (n - 1) == 0:
        return index ^ step
    return lax.rem(index - step + n, n)


def target(index, step, n):
    if n & (n - 1) == 0:
        return index ^ step
    return lax.rem(index + step, n)


def depth_cuts(depth):
    half = max(256, (depth // 2 + 255) // 256 * 256)
    return [(0, half), (half, depth)] if half < depth else [(0, depth)]


def partial_kernel(n_space, cuts, v_ref, s_ref, *rest):
    outs = rest[:n_space]
    v_buf, s_buf, acc, in_sem = rest[n_space:]
    _, nt, nev, _ = v_ref.shape
    _, _, nsp, nj, _ = s_ref.shape
    copies = []
    for t in range(nt):
        for c, (lo, hi) in enumerate(cuts):
            group = []
            for p in range(2):
                group += [
                    pltpu.make_async_copy(
                        v_ref.at[p, t, :, lo:hi], v_buf.at[p, t, :, lo:hi], in_sem.at[t, c, 2 * p]
                    ),
                    pltpu.make_async_copy(
                        s_ref.at[p, t, :, :, lo:hi],
                        s_buf.at[p, t, :, :, lo:hi],
                        in_sem.at[t, c, 2 * p + 1],
                    ),
                ]
            for copy in group:
                copy.start()
            copies.append(group)
    for t in range(nt):
        total = None
        for c, (lo, hi) in enumerate(cuts):
            for copy in copies[t * len(cuts) + c]:
                copy.wait()
            vr, vi = v_buf[0, t, :, lo:hi], v_buf[1, t, :, lo:hi]
            sr = s_buf[0, t, :, :, lo:hi].reshape(nsp * nj, hi - lo)
            si = s_buf[1, t, :, :, lo:hi].reshape(nsp * nj, hi - lo)
            both = dot(jnp.concatenate([sr, si]), vr, NT_DOT) + dot(
                jnp.concatenate([si, -sr]), vi, NT_DOT
            )
            total = both if total is None else total + both
        total = total.reshape(2, nsp, nj, nev)
        for sp in range(nsp):
            for p in range(2):
                start = ((t * nsp + sp) * 2 + p) * nj
                acc[start : start + nj, :] = total[p, sp]
    chunk = acc.shape[0] // n_space
    me = lax.axis_index("space")
    for s in range(n_space):
        rows = pl.ds(pl.multiple_of(target(me, s, n_space) * chunk, chunk), chunk)
        outs[s][...] = acc[rows, :].astype(outs[s].dtype)


def partial_taus(eigvecs, solutions, n_space, send_type):
    _, nt, nev, depth = eigvecs.shape
    _, _, nsp, nj, _ = solutions.shape
    rows = nt * nsp * 2 * nj
    cuts = depth_cuts(depth)
    chunk = (rows // n_space, nev)
    return pl.pallas_call(
        functools.partial(partial_kernel, n_space, cuts),
        out_shape=[pltpu.VMEM(chunk, jnp.float32)] + [pltpu.VMEM(chunk, send_type)] * (n_space - 1),
        in_specs=[pl.BlockSpec(memory_space=pl.ANY)] * 2,
        out_specs=[pl.BlockSpec(memory_space=pltpu.VMEM)] * n_space,
        scratch_shapes=[
            pltpu.VMEM(eigvecs.shape, eigvecs.dtype),
            pltpu.VMEM(solutions.shape, solutions.dtype),
            pltpu.VMEM((rows, nev), jnp.float32),
            pltpu.SemaphoreType.DMA((nt, len(cuts), 4)),
        ],
        compiler_params=pltpu.CompilerParams(vmem_limit_bytes=32 * 2**20),
        cost_estimate=pl.CostEstimate(
            flops=4 * rows * nev * depth,
            bytes_accessed=2 * (eigvecs.size + solutions.size) + 4 * rows * nev,
            transcendentals=0,
        ),
    )(
        pltpu.with_memory_space_constraint(eigvecs, pltpu.HBM),
        pltpu.with_memory_space_constraint(solutions, pltpu.HBM),
    )


def contract_kernel(layout, firsts, per_chunk, group, item_in, live_in, elems, *rest):
    n_space, n_spin, n_cons, nt, nsp, nj = layout
    n_parts = len(firsts)
    parts, out_ref = rest[:n_parts], rest[n_parts]
    tau, outs, mid, item_ref, live_ref, out_sem, slot_sem = rest[n_parts + 1 :]
    unit, nev = tau.shape[-2:]
    slots = out_ref.shape[1]
    scale = nev ** (-0.5)
    space, spin, cons = (lax.axis_index(a) for a in ("space", "spin", "cons"))
    loads = [
        pltpu.make_async_copy(item_in, item_ref, slot_sem.at[0]),
        pltpu.make_async_copy(live_in, live_ref, slot_sem.at[1]),
    ]
    for copy in loads:
        copy.start()
    for part, first in zip(parts, firsts):
        tau[first : first + part.shape[0]] = part[...]
    for copy in loads:
        copy.wait()

    def matrix(t, a, p):
        first = ((t * nsp + a % nsp) * 2 + p) * (nj // unit)
        rows = []
        for z in range(n_cons):
            z_step = step_from(z, cons, n_cons)
            for k in range(nj // unit):
                where = first + k
                step = step_from(where // per_chunk, space, n_space)
                part = step_from(a // nsp, spin, n_spin) * n_space + step
                rows.append(tau[(part * n_cons + z_step) * per_chunk + where % per_chunk])
        return jnp.concatenate(rows)

    def write(k):
        return pltpu.make_async_copy(outs.at[k], out_ref.at[:, k], out_sem.at[k])

    def right_half(u, item):
        e, _, b, t = item
        er, ei = elems[e, 0], elems[e, 1]
        tau_b = jnp.concatenate([matrix(t, b, 0), matrix(t, b, 1)], axis=1)
        real = dot(jnp.concatenate([er, -ei], axis=1), tau_b, NT_DOT)
        imag = dot(jnp.concatenate([ei, er], axis=1), tau_b, NT_DOT)
        mid[u, :nev] = real.astype(mid.dtype)
        mid[u, nev:] = imag.astype(mid.dtype)

    def left_half(u, k, item):
        _, a, _, t = item
        ar, ai = matrix(t, a, 0), matrix(t, a, 1)
        keep = k < live_ref[0]
        real = dot(jnp.concatenate([ar, ai], axis=1), mid[u], NN_DOT)
        imag = dot(jnp.concatenate([-ai, ar], axis=1), mid[u], NN_DOT)
        outs[k, 0] = jnp.where(keep, real * scale, 0.0).astype(outs.dtype)
        outs[k, 1] = jnp.where(keep, imag * scale, 0.0).astype(outs.dtype)

    def slots_from(first, size):
        ks = [first + u for u in range(size)]
        items = [tuple(item_ref[n, k] for n in range(4)) for k in ks]
        right_half(0, items[0])
        for u in range(size):
            if u + 1 < size:
                right_half(u + 1, items[u + 1])
            left_half(u, ks[u], items[u])
            write(ks[u]).start()

    def empty(k, carry):
        outs[k] = jnp.zeros(outs.shape[1:], outs.dtype)
        write(k).start()
        return carry

    def large(g, carry):
        slots_from(g * 2 * group, 2 * group)
        return carry

    def small(g, carry):
        slots_from(g * group, group)
        return carry

    pairs = lax.div(live_ref[0], 2 * group)
    used = lax.div(live_ref[0] + group - 1, group)
    lax.fori_loop(used * group, slots, empty, 0)
    lax.fori_loop(0, pairs, large, 0)
    lax.fori_loop(2 * pairs, used, small, 0)
    for k in range(slots):
        write(k).wait()


def step_from(sender, me, n):
    if n & (n - 1) == 0:
        return sender ^ me
    return lax.rem(me - sender + n, n)


def contract(items, live, elementals, parts, firsts, layout):
    n_space, n_spin, n_cons, nt, nsp, nj = layout
    slots = items.shape[1]
    nev = elementals.shape[-1]
    chunk = nt * nsp * 2 * nj // n_space
    unit = min(chunk, nj)
    group = math.gcd(slots, 4)
    parts = [part.reshape(-1, unit, nev) for part in parts]
    firsts = [first // unit for first in firsts]
    return pl.pallas_call(
        functools.partial(contract_kernel, layout, firsts, chunk // unit, group),
        out_shape=jax.ShapeDtypeStruct((2, slots, nev, nev), jnp.bfloat16),
        in_specs=[pl.BlockSpec(memory_space=pl.ANY)] * 2
        + [pl.BlockSpec(memory_space=pltpu.VMEM)] * (1 + len(parts)),
        out_specs=pl.BlockSpec(memory_space=pl.ANY),
        scratch_shapes=[
            pltpu.VMEM((n_space * n_spin * n_cons * chunk // unit, unit, nev), jnp.bfloat16),
            pltpu.VMEM((slots, 2, nev, nev), jnp.bfloat16),
            pltpu.VMEM((2 * group, 2 * nev, nev), jnp.bfloat16),
            pltpu.SMEM(items.shape, jnp.int32),
            pltpu.SMEM(live.shape, jnp.int32),
            pltpu.SemaphoreType.DMA((slots,)),
            pltpu.SemaphoreType.DMA((2,)),
        ],
        compiler_params=pltpu.CompilerParams(vmem_limit_bytes=32 * 2**20),
        cost_estimate=pl.CostEstimate(
            flops=16 * slots * nev**3,
            bytes_accessed=2 * (elementals.size + 2 * slots * nev * nev),
            transcendentals=0,
        ),
    )(
        items,
        live,
        *(pltpu.with_memory_space_constraint(x, pltpu.VMEM) for x in [elementals] + parts),
    )


def body(eigvecs, solutions, elementals, op_list, live_count):
    n_space, n_spin, n_cons = (lax.axis_size(a) for a in ("space", "spin", "cons"))
    _, nt, nev, _ = eigvecs.shape
    _, _, nsp, nj, _ = solutions.shape
    sends = partial_taus(eigvecs, solutions, n_space, jnp.float32)
    elementals, sends = lax.optimization_barrier((elementals, sends))
    space_steps, spin_steps, cons_steps = partners(n_space), partners(n_spin), partners(n_cons)

    def over_space(x, s):
        return lax.ppermute(x, "space", space_steps[s])

    def over_cons(x, s):
        return lax.ppermute(x, "cons", cons_steps[s])

    got = [sends[0]] + [over_space(sends[s], s) for s in range(1, n_space)[::-1]]
    mine = functools.reduce(jnp.add, [part.astype(jnp.float32) for part in got])
    mine = mine.astype(jnp.bfloat16)
    pieces = [mine] + [over_cons(mine, s) for s in range(1, n_cons)]
    own = jnp.stack(pieces).reshape(-1, nev)
    rows = own.shape[0]

    far = []
    if n_space == 4:
        across = n_space - 1
        first = over_space(mine, across)
        own, first = lax.optimization_barrier((own, first))
        place = across * rows
        height = mine.shape[0]
        rest = over_space(jnp.stack(pieces[2:]).reshape(-1, nev), across)
        far = [(jnp.stack([first, over_cons(first, 1)]).reshape(-1, nev), place), (rest, place + 2 * height)]
    near = range(1, n_space - 1 if far else n_space)
    held = [(own, 0)] + far + [(over_space(own, s), s * rows) for s in near]
    for c in range(1, n_spin):
        held += [
            (lax.ppermute(part, "spin", spin_steps[c]), c * n_space * rows + place)
            for part, place in held[: len(far) + len(near) + 1]
        ]
    layout = (n_space, n_spin, n_cons, nt, nsp, nj)
    return contract(op_list[0].T, live_count, elementals, *zip(*held), layout)


def solution(mesh):
    return jax.shard_map(
        body,
        mesh=mesh,
        in_specs=(
            P(None, None, None, "space"),
            P(None, None, "spin", "cons", "space"),
            P(),
            P(("space", "spin", "cons"), None, None),
            P(("space", "spin", "cons")),
        ),
        out_specs=P(None, ("space", "spin", "cons"), None, None),
        check_vma=False,
    )
```

```python
import functools
import math

import jax
import jax.numpy as jnp
from jax import lax
from jax.experimental import pallas as pl
from jax.experimental.pallas import tpu as pltpu
from jax.sharding import PartitionSpec as P

NT_DOT = (((1,), (1,)), ((), ()))
NN_DOT = (((1,), (0,)), ((), ()))


dot = functools.partial(lax.dot_general, preferred_element_type=jnp.float32)


def partners(n):
    if n & (n - 1) == 0:
        return [[(i, i ^ s) for i in range(n)] for s in range(n)]
    return [[(i, (i + s) % n) for i in range(n)] for s in range(n)]


def partner(index, step, n):
    if n & (n - 1) == 0:
        return index ^ step
    return lax.rem(index - step + n, n)


def target(index, step, n):
    if n & (n - 1) == 0:
        return index ^ step
    return lax.rem(index + step, n)


def depth_cuts(depth):
    half = max(256, (depth // 2 + 255) // 256 * 256)
    return [(0, half), (half, depth)] if half < depth else [(0, depth)]


def partial_kernel(n_space, cuts, v_ref, s_ref, *rest):
    outs = rest[:n_space]
    v_buf, s_buf, acc, in_sem = rest[n_space:]
    _, nt, nev, _ = v_ref.shape
    _, _, nsp, nj, _ = s_ref.shape
    copies = []
    for t in range(nt):
        for c, (lo, hi) in enumerate(cuts):
            group = []
            for p in range(2):
                group += [
                    pltpu.make_async_copy(
                        v_ref.at[p, t, :, lo:hi], v_buf.at[p, t, :, lo:hi], in_sem.at[t, c, 2 * p]
                    ),
                    pltpu.make_async_copy(
                        s_ref.at[p, t, :, :, lo:hi],
                        s_buf.at[p, t, :, :, lo:hi],
                        in_sem.at[t, c, 2 * p + 1],
                    ),
                ]
            for copy in group:
                copy.start()
            copies.append(group)
    for t in range(nt):
        total = None
        for c, (lo, hi) in enumerate(cuts):
            for copy in copies[t * len(cuts) + c]:
                copy.wait()
            vr, vi = v_buf[0, t, :, lo:hi], v_buf[1, t, :, lo:hi]
            sr = s_buf[0, t, :, :, lo:hi].reshape(nsp * nj, hi - lo)
            si = s_buf[1, t, :, :, lo:hi].reshape(nsp * nj, hi - lo)
            both = dot(jnp.concatenate([sr, si]), vr, NT_DOT) + dot(
                jnp.concatenate([si, -sr]), vi, NT_DOT
            )
            total = both if total is None else total + both
        total = total.reshape(2, nsp, nj, nev)
        for sp in range(nsp):
            for p in range(2):
                start = ((t * nsp + sp) * 2 + p) * nj
                acc[start : start + nj, :] = total[p, sp]
    chunk = acc.shape[0] // n_space
    me = lax.axis_index("space")
    for s in range(n_space):
        rows = pl.ds(pl.multiple_of(target(me, s, n_space) * chunk, chunk), chunk)
        outs[s][...] = acc[rows, :].astype(outs[s].dtype)


def partial_taus(eigvecs, solutions, n_space, send_type):
    _, nt, nev, depth = eigvecs.shape
    _, _, nsp, nj, _ = solutions.shape
    rows = nt * nsp * 2 * nj
    cuts = depth_cuts(depth)
    chunk = (rows // n_space, nev)
    return pl.pallas_call(
        functools.partial(partial_kernel, n_space, cuts),
        out_shape=[pltpu.VMEM(chunk, jnp.float32)] + [pltpu.VMEM(chunk, send_type)] * (n_space - 1),
        in_specs=[pl.BlockSpec(memory_space=pl.ANY)] * 2,
        out_specs=[pl.BlockSpec(memory_space=pltpu.VMEM)] * n_space,
        scratch_shapes=[
            pltpu.VMEM(eigvecs.shape, eigvecs.dtype),
            pltpu.VMEM(solutions.shape, solutions.dtype),
            pltpu.VMEM((rows, nev), jnp.float32),
            pltpu.SemaphoreType.DMA((nt, len(cuts), 4)),
        ],
        compiler_params=pltpu.CompilerParams(vmem_limit_bytes=32 * 2**20),
        cost_estimate=pl.CostEstimate(
            flops=4 * rows * nev * depth,
            bytes_accessed=2 * (eigvecs.size + solutions.size) + 4 * rows * nev,
            transcendentals=0,
        ),
    )(
        pltpu.with_memory_space_constraint(eigvecs, pltpu.HBM),
        pltpu.with_memory_space_constraint(solutions, pltpu.HBM),
    )


def contract_kernel(layout, firsts, per_chunk, group, item_in, live_in, elems, *rest):
    n_space, n_spin, n_cons, nt, nsp, nj = layout
    n_parts = len(firsts)
    parts, out_ref = rest[:n_parts], rest[n_parts]
    tau, outs, mid, item_ref, live_ref, out_sem, slot_sem = rest[n_parts + 1 :]
    unit, nev = tau.shape[-2:]
    slots = out_ref.shape[1]
    scale = nev ** (-0.5)
    space, spin, cons = (lax.axis_index(a) for a in ("space", "spin", "cons"))
    loads = [
        pltpu.make_async_copy(item_in, item_ref, slot_sem.at[0]),
        pltpu.make_async_copy(live_in, live_ref, slot_sem.at[1]),
    ]
    for copy in loads:
        copy.start()
    for part, first in zip(parts, firsts):
        tau[first : first + part.shape[0]] = part[...]
    for copy in loads:
        copy.wait()

    def matrix(t, a, p):
        first = ((t * nsp + a % nsp) * 2 + p) * (nj // unit)
        rows = []
        for z in range(n_cons):
            z_step = step_from(z, cons, n_cons)
            for k in range(nj // unit):
                where = first + k
                step = step_from(where // per_chunk, space, n_space)
                part = step_from(a // nsp, spin, n_spin) * n_space + step
                rows.append(tau[(part * n_cons + z_step) * per_chunk + where % per_chunk])
        return jnp.concatenate(rows)

    def write(k):
        return pltpu.make_async_copy(outs.at[k], out_ref.at[:, k], out_sem.at[k])

    def right_half(u, item):
        e, _, b, t = item
        er, ei = elems[e, 0], elems[e, 1]
        tau_b = jnp.concatenate([matrix(t, b, 0), matrix(t, b, 1)], axis=1)
        real = dot(jnp.concatenate([er, -ei], axis=1), tau_b, NT_DOT)
        imag = dot(jnp.concatenate([ei, er], axis=1), tau_b, NT_DOT)
        mid[u, :nev] = real.astype(mid.dtype)
        mid[u, nev:] = imag.astype(mid.dtype)

    def left_half(u, k, item):
        _, a, _, t = item
        ar, ai = matrix(t, a, 0), matrix(t, a, 1)
        keep = k < live_ref[0]
        real = dot(jnp.concatenate([ar, ai], axis=1), mid[u], NN_DOT)
        imag = dot(jnp.concatenate([-ai, ar], axis=1), mid[u], NN_DOT)
        outs[k, 0] = jnp.where(keep, real * scale, 0.0).astype(outs.dtype)
        outs[k, 1] = jnp.where(keep, imag * scale, 0.0).astype(outs.dtype)

    def slots_from(first, size):
        ks = [first + u for u in range(size)]
        items = [tuple(item_ref[n, k] for n in range(4)) for k in ks]
        right_half(0, items[0])
        for u in range(size):
            if u + 1 < size:
                right_half(u + 1, items[u + 1])
            left_half(u, ks[u], items[u])
            write(ks[u]).start()

    def empty(k, carry):
        outs[k] = jnp.zeros(outs.shape[1:], outs.dtype)
        write(k).start()
        return carry

    def large(g, carry):
        slots_from(g * 4 * group, 4 * group)
        return carry

    def small(g, carry):
        slots_from(g * group, group)
        return carry

    blocks = lax.div(live_ref[0], 4 * group)
    used = lax.div(live_ref[0] + group - 1, group)
    lax.fori_loop(used * group, slots, empty, 0)
    lax.fori_loop(0, blocks, large, 0)
    lax.fori_loop(4 * blocks, used, small, 0)
    for k in range(slots):
        write(k).wait()


def step_from(sender, me, n):
    if n & (n - 1) == 0:
        return sender ^ me
    return lax.rem(me - sender + n, n)


def contract(items, live, elementals, parts, firsts, layout):
    n_space, n_spin, n_cons, nt, nsp, nj = layout
    slots = items.shape[1]
    nev = elementals.shape[-1]
    chunk = nt * nsp * 2 * nj // n_space
    unit = min(chunk, nj)
    group = math.gcd(slots, 2)
    parts = [part.reshape(-1, unit, nev) for part in parts]
    firsts = [first // unit for first in firsts]
    return pl.pallas_call(
        functools.partial(contract_kernel, layout, firsts, chunk // unit, group),
        out_shape=jax.ShapeDtypeStruct((2, slots, nev, nev), jnp.bfloat16),
        in_specs=[pl.BlockSpec(memory_space=pl.ANY)] * 2
        + [pl.BlockSpec(memory_space=pltpu.VMEM)] * (1 + len(parts)),
        out_specs=pl.BlockSpec(memory_space=pl.ANY),
        scratch_shapes=[
            pltpu.VMEM((n_space * n_spin * n_cons * chunk // unit, unit, nev), jnp.bfloat16),
            pltpu.VMEM((slots, 2, nev, nev), jnp.bfloat16),
            pltpu.VMEM((4 * group, 2 * nev, nev), jnp.bfloat16),
            pltpu.SMEM(items.shape, jnp.int32),
            pltpu.SMEM(live.shape, jnp.int32),
            pltpu.SemaphoreType.DMA((slots,)),
            pltpu.SemaphoreType.DMA((2,)),
        ],
        compiler_params=pltpu.CompilerParams(vmem_limit_bytes=32 * 2**20),
        cost_estimate=pl.CostEstimate(
            flops=16 * slots * nev**3,
            bytes_accessed=2 * (elementals.size + 2 * slots * nev * nev),
            transcendentals=0,
        ),
    )(
        items,
        live,
        *(pltpu.with_memory_space_constraint(x, pltpu.VMEM) for x in [elementals] + parts),
    )


def body(eigvecs, solutions, elementals, op_list, live_count):
    n_space, n_spin, n_cons = (lax.axis_size(a) for a in ("space", "spin", "cons"))
    _, nt, nev, _ = eigvecs.shape
    _, _, nsp, nj, _ = solutions.shape
    sends = partial_taus(eigvecs, solutions, n_space, jnp.bfloat16)
    elementals, sends = lax.optimization_barrier((elementals, sends))
    space_steps, spin_steps, cons_steps = partners(n_space), partners(n_spin), partners(n_cons)

    def over_space(x, s):
        return lax.ppermute(x, "space", space_steps[s])

    def over_cons(x, s):
        return lax.ppermute(x, "cons", cons_steps[s])

    got = [sends[0]] + [over_space(sends[s], s) for s in range(1, n_space)[::-1]]
    mine = functools.reduce(jnp.add, [part.astype(jnp.float32) for part in got])
    mine = mine.astype(jnp.bfloat16)
    pieces = [mine] + [over_cons(mine, s) for s in range(1, n_cons)]
    own = jnp.stack(pieces).reshape(-1, nev)
    rows = own.shape[0]

    far = []
    if n_space == 4:
        across = n_space - 1
        first = over_space(mine, across)
        own, first = lax.optimization_barrier((own, first))
        place = across * rows
        height = mine.shape[0]
        rest = over_space(jnp.stack(pieces[2:]).reshape(-1, nev), across)
        far = [(jnp.stack([first, over_cons(first, 1)]).reshape(-1, nev), place), (rest, place + 2 * height)]
    near = range(1, n_space - 1 if far else n_space)
    held = [(own, 0)] + far + [(over_space(own, s), s * rows) for s in near]
    for c in range(1, n_spin):
        held += [
            (lax.ppermute(part, "spin", spin_steps[c]), c * n_space * rows + place)
            for part, place in held[: len(far) + len(near) + 1]
        ]
    layout = (n_space, n_spin, n_cons, nt, nsp, nj)
    return contract(op_list[0].T, live_count, elementals, *zip(*held), layout)


def solution(mesh):
    return jax.shard_map(
        body,
        mesh=mesh,
        in_specs=(
            P(None, None, None, "space"),
            P(None, None, "spin", "cons", "space"),
            P(),
            P(("space", "spin", "cons"), None, None),
            P(("space", "spin", "cons")),
        ),
        out_specs=P(None, ("space", "spin", "cons"), None, None),
        check_vma=False,
    )
```

```python
import functools
import math

import jax
import jax.numpy as jnp
from jax import lax
from jax.experimental import pallas as pl
from jax.experimental.pallas import tpu as pltpu
from jax.sharding import PartitionSpec as P

NT_DOT = (((1,), (1,)), ((), ()))
NN_DOT = (((1,), (0,)), ((), ()))


dot = functools.partial(lax.dot_general, preferred_element_type=jnp.float32)


def partners(n):
    if n & (n - 1) == 0:
        return [[(i, i ^ s) for i in range(n)] for s in range(n)]
    return [[(i, (i + s) % n) for i in range(n)] for s in range(n)]


def partner(index, step, n):
    if n & (n - 1) == 0:
        return index ^ step
    return lax.rem(index - step + n, n)


def target(index, step, n):
    if n & (n - 1) == 0:
        return index ^ step
    return lax.rem(index + step, n)


def depth_cuts(depth):
    half = max(256, (depth // 2 + 255) // 256 * 256)
    return [(0, half), (half, depth)] if half < depth else [(0, depth)]


def partial_kernel(n_space, cuts, v_ref, s_ref, *rest):
    outs = rest[:n_space]
    v_buf, s_buf, acc, in_sem = rest[n_space:]
    _, nt, nev, _ = v_ref.shape
    _, _, nsp, nj, _ = s_ref.shape
    copies = []
    for t in range(nt):
        for c, (lo, hi) in enumerate(cuts):
            group = []
            for p in range(2):
                group += [
                    pltpu.make_async_copy(
                        v_ref.at[p, t, :, lo:hi], v_buf.at[p, t, :, lo:hi], in_sem.at[t, c, 2 * p]
                    ),
                    pltpu.make_async_copy(
                        s_ref.at[p, t, :, :, lo:hi],
                        s_buf.at[p, t, :, :, lo:hi],
                        in_sem.at[t, c, 2 * p + 1],
                    ),
                ]
            for copy in group:
                copy.start()
            copies.append(group)
    for t in range(nt):
        total = None
        for c, (lo, hi) in enumerate(cuts):
            for copy in copies[t * len(cuts) + c]:
                copy.wait()
            vr, vi = v_buf[0, t, :, lo:hi], v_buf[1, t, :, lo:hi]
            sr = s_buf[0, t, :, :, lo:hi].reshape(nsp * nj, hi - lo)
            si = s_buf[1, t, :, :, lo:hi].reshape(nsp * nj, hi - lo)
            both = dot(jnp.concatenate([sr, si]), vr, NT_DOT) + dot(
                jnp.concatenate([si, -sr]), vi, NT_DOT
            )
            total = both if total is None else total + both
        total = total.reshape(2, nsp, nj, nev)
        for sp in range(nsp):
            for p in range(2):
                start = ((t * nsp + sp) * 2 + p) * nj
                acc[start : start + nj, :] = total[p, sp]
    chunk = acc.shape[0] // n_space
    me = lax.axis_index("space")
    for s in range(n_space):
        rows = pl.ds(pl.multiple_of(target(me, s, n_space) * chunk, chunk), chunk)
        outs[s][...] = acc[rows, :].astype(outs[s].dtype)


def partial_taus(eigvecs, solutions, n_space, send_type):
    _, nt, nev, depth = eigvecs.shape
    _, _, nsp, nj, _ = solutions.shape
    rows = nt * nsp * 2 * nj
    cuts = depth_cuts(depth)
    chunk = (rows // n_space, nev)
    return pl.pallas_call(
        functools.partial(partial_kernel, n_space, cuts),
        out_shape=[pltpu.VMEM(chunk, jnp.float32)] + [pltpu.VMEM(chunk, send_type)] * (n_space - 1),
        in_specs=[pl.BlockSpec(memory_space=pl.ANY)] * 2,
        out_specs=[pl.BlockSpec(memory_space=pltpu.VMEM)] * n_space,
        scratch_shapes=[
            pltpu.VMEM(eigvecs.shape, eigvecs.dtype),
            pltpu.VMEM(solutions.shape, solutions.dtype),
            pltpu.VMEM((rows, nev), jnp.float32),
            pltpu.SemaphoreType.DMA((nt, len(cuts), 4)),
        ],
        compiler_params=pltpu.CompilerParams(vmem_limit_bytes=32 * 2**20),
        cost_estimate=pl.CostEstimate(
            flops=4 * rows * nev * depth,
            bytes_accessed=2 * (eigvecs.size + solutions.size) + 4 * rows * nev,
            transcendentals=0,
        ),
    )(
        pltpu.with_memory_space_constraint(eigvecs, pltpu.HBM),
        pltpu.with_memory_space_constraint(solutions, pltpu.HBM),
    )


def contract_kernel(layout, firsts, per_chunk, group, item_in, live_in, elems, *rest):
    n_space, n_spin, n_cons, nt, nsp, nj = layout
    n_parts = len(firsts)
    parts, out_ref = rest[:n_parts], rest[n_parts]
    tau, outs, mid, item_ref, live_ref, out_sem, slot_sem = rest[n_parts + 1 :]
    unit, nev = tau.shape[-2:]
    slots = out_ref.shape[1]
    scale = nev ** (-0.5)
    space, spin, cons = (lax.axis_index(a) for a in ("space", "spin", "cons"))
    loads = [
        pltpu.make_async_copy(item_in, item_ref, slot_sem.at[0]),
        pltpu.make_async_copy(live_in, live_ref, slot_sem.at[1]),
    ]
    for copy in loads:
        copy.start()
    for part, first in zip(parts, firsts):
        tau[first : first + part.shape[0]] = part[...]
    for copy in loads:
        copy.wait()

    def matrix(t, a, p):
        first = ((t * nsp + a % nsp) * 2 + p) * (nj // unit)
        rows = []
        for z in range(n_cons):
            z_step = step_from(z, cons, n_cons)
            for k in range(nj // unit):
                where = first + k
                step = step_from(where // per_chunk, space, n_space)
                part = step_from(a // nsp, spin, n_spin) * n_space + step
                rows.append(tau[(part * n_cons + z_step) * per_chunk + where % per_chunk])
        return jnp.concatenate(rows)

    def write(k):
        return pltpu.make_async_copy(outs.at[k], out_ref.at[:, k], out_sem.at[k])

    def right_half(u, item):
        e, _, b, t = item
        er, ei = elems[e, 0], elems[e, 1]
        tau_b = jnp.concatenate([matrix(t, b, 0), matrix(t, b, 1)], axis=1)
        real = dot(jnp.concatenate([er, -ei], axis=1), tau_b, NT_DOT)
        imag = dot(jnp.concatenate([ei, er], axis=1), tau_b, NT_DOT)
        mid[u, :nev] = real.astype(mid.dtype)
        mid[u, nev:] = imag.astype(mid.dtype)

    def left_half(u, k, item):
        _, a, _, t = item
        ar, ai = matrix(t, a, 0), matrix(t, a, 1)
        keep = k < live_ref[0]
        real = dot(jnp.concatenate([ar, ai], axis=1), mid[u], NN_DOT)
        imag = dot(jnp.concatenate([-ai, ar], axis=1), mid[u], NN_DOT)
        outs[k, 0] = jnp.where(keep, real * scale, 0.0).astype(outs.dtype)
        outs[k, 1] = jnp.where(keep, imag * scale, 0.0).astype(outs.dtype)

    def slots_from(first, size):
        ks = [first + u for u in range(size)]
        items = [tuple(item_ref[n, k] for n in range(4)) for k in ks]
        right_half(0, items[0])
        for u in range(size):
            if u + 1 < size:
                right_half(u + 1, items[u + 1])
            left_half(u, ks[u], items[u])
            write(ks[u]).start()

    def empty(k, carry):
        outs[k] = jnp.zeros(outs.shape[1:], outs.dtype)
        write(k).start()
        return carry

    def large(g, carry):
        slots_from(g * 4 * group, 4 * group)
        return carry

    def small(g, carry):
        slots_from(g * group, group)
        return carry

    blocks = lax.div(live_ref[0], 4 * group)
    used = lax.div(live_ref[0] + group - 1, group)
    lax.fori_loop(used * group, slots, empty, 0)
    lax.fori_loop(0, blocks, large, 0)
    lax.fori_loop(4 * blocks, used, small, 0)
    for k in range(slots):
        write(k).wait()


def step_from(sender, me, n):
    if n & (n - 1) == 0:
        return sender ^ me
    return lax.rem(me - sender + n, n)


def contract(items, live, elementals, parts, firsts, layout):
    n_space, n_spin, n_cons, nt, nsp, nj = layout
    slots = items.shape[1]
    nev = elementals.shape[-1]
    chunk = nt * nsp * 2 * nj // n_space
    unit = min(chunk, nj)
    group = math.gcd(slots, 2)
    parts = [part.reshape(-1, unit, nev) for part in parts]
    firsts = [first // unit for first in firsts]
    return pl.pallas_call(
        functools.partial(contract_kernel, layout, firsts, chunk // unit, group),
        out_shape=jax.ShapeDtypeStruct((2, slots, nev, nev), jnp.bfloat16),
        in_specs=[pl.BlockSpec(memory_space=pl.ANY)] * 2
        + [pl.BlockSpec(memory_space=pltpu.VMEM)] * (1 + len(parts)),
        out_specs=pl.BlockSpec(memory_space=pl.ANY),
        scratch_shapes=[
            pltpu.VMEM((n_space * n_spin * n_cons * chunk // unit, unit, nev), jnp.bfloat16),
            pltpu.VMEM((slots, 2, nev, nev), jnp.bfloat16),
            pltpu.VMEM((4 * group, 2 * nev, nev), jnp.bfloat16),
            pltpu.SMEM(items.shape, jnp.int32),
            pltpu.SMEM(live.shape, jnp.int32),
            pltpu.SemaphoreType.DMA((slots,)),
            pltpu.SemaphoreType.DMA((2,)),
        ],
        compiler_params=pltpu.CompilerParams(vmem_limit_bytes=32 * 2**20),
        cost_estimate=pl.CostEstimate(
            flops=16 * slots * nev**3,
            bytes_accessed=2 * (elementals.size + 2 * slots * nev * nev),
            transcendentals=0,
        ),
    )(
        items,
        live,
        *(pltpu.with_memory_space_constraint(x, pltpu.VMEM) for x in [elementals] + parts),
    )


def body(eigvecs, solutions, elementals, op_list, live_count):
    n_space, n_spin, n_cons = (lax.axis_size(a) for a in ("space", "spin", "cons"))
    _, nt, nev, _ = eigvecs.shape
    _, _, nsp, nj, _ = solutions.shape
    sends = partial_taus(eigvecs, solutions, n_space, jnp.bfloat16)
    elementals, sends = lax.optimization_barrier((elementals, sends))
    space_steps, spin_steps, cons_steps = partners(n_space), partners(n_spin), partners(n_cons)

    def over_space(x, s):
        return lax.ppermute(x, "space", space_steps[s])

    def over_cons(x, s):
        return lax.ppermute(x, "cons", cons_steps[s])

    got = [sends[0]] + [over_space(sends[s], s) for s in range(1, n_space)[::-1]]
    mine = functools.reduce(jnp.add, [part.astype(jnp.float32) for part in got])
    mine = mine.astype(jnp.bfloat16)
    pieces = [mine] + [over_cons(mine, s) for s in range(1, n_cons)]
    own = jnp.stack(pieces).reshape(-1, nev)
    rows = own.shape[0]

    far = []
    if n_space == 4:
        across = n_space - 1
        first = over_space(mine, across)
        own_late, first = lax.optimization_barrier((own, first))
        place = across * rows
        height = mine.shape[0]
        rest = over_space(jnp.stack(pieces[2:]).reshape(-1, nev), across)
        far = [(jnp.stack([first, over_cons(first, 1)]).reshape(-1, nev), place), (rest, place + 2 * height)]
    near = range(1, n_space - 1 if far else n_space)[::-1]
    held = [(own, 0)] + far + [(over_space(own_late if far and s == 2 else own, s), s * rows) for s in near]
    for c in range(1, n_spin):
        held += [
            (lax.ppermute(part, "spin", spin_steps[c]), c * n_space * rows + place)
            for part, place in held[: len(far) + len(near) + 1]
        ]
    layout = (n_space, n_spin, n_cons, nt, nsp, nj)
    return contract(op_list[0].T, live_count, elementals, *zip(*held), layout)


def solution(mesh):
    return jax.shard_map(
        body,
        mesh=mesh,
        in_specs=(
            P(None, None, None, "space"),
            P(None, None, "spin", "cons", "space"),
            P(),
            P(("space", "spin", "cons"), None, None),
            P(("space", "spin", "cons")),
        ),
        out_specs=P(None, ("space", "spin", "cons"), None, None),
        check_vma=False,
    )
```
